1024 devices in a mesh: ctx: 64 (over y, z_lo), tp: 16 (over x, z_hi, core).
Axes of the slice: x: 4, y: 8, z: 16 (z_hi: 2, z_lo: 8; z = z_hi * 8 + z_lo), core: 2. Of those that a mesh axis runs over, the one named last changes fastest.
Arguments:
- queries: bfloat16 [8192, 8192], P('ctx', 'tp'), may hold values from -6 to 6
- keys: bfloat16 [8192, 8192], P('ctx', 'tp'), may hold values from -6 to 6
- values: bfloat16 [8192, 8192], P('ctx', 'tp'), may hold values from -6 to 6
- short_taps: float32 [3, 3, 8192], P(None, None, 'tp'), may hold values from -3.5 to 3.5
- long_rates: float32 [8192, 16], P('tp'), may hold values from 2.4414062e-06 to 0.05
- long_resid: float32 [8192, 16], P('tp'), may hold values from -1.5 to 1.5
- out_weight: bfloat16 [8192, 4096], P('tp'), may hold values from -0.09375 to 0.09375
Outputs:
- block_out: bfloat16 [8192, 4096], P('ctx', 'tp')
The draws below stay inside these ranges and needn't reach their ends.
All inputs are finite; a program needn't handle non-finite values.
Results may differ from the reference program's by a relative error of at most 0.017.
Values may be sent and summed in bfloat16 or wider, within the bound.
A program may use at most 128 MiB of HBM per device.

```python
import math
import jax
import jax.numpy as jnp
from jax import lax

D = 8192
OUT = 4096
MODES = 16
SHORT = 3
SEQ = 8192


def raised(array, stream_key, source, target, parts, factor):
    owner, partner = [(jnp.arange(array.shape[position]) // (array.shape[position] // parts)).reshape([-1 if axis == position else 1 for axis in range(array.ndim)]) for position in (source, target)]
    chosen = jax.random.permutation(stream_key, parts)[partner]
    strong = (owner == chosen) | (owner == (partner + parts // 2) % parts)
    return jnp.where(strong, factor * array, array)


def steps_of(key, extent, split, least, top_value):
    loudness, own = 1.0, jax.random.fold_in(key, 6)
    for position, shards_of in split:
        steps = jnp.exp(jax.random.uniform(jax.random.fold_in(own, position), (shards_of,), jnp.float32, least / len(split), top_value / len(split)))
        loudness = loudness * jnp.repeat(steps, extent[position] // shards_of).reshape([-1 if axis == position else 1 for axis in range(len(extent))])
    return loudness


def scatter_about(rng, dims, scale, limit, split=(), kind=jnp.bfloat16):
    drawn = scale * jax.random.normal(rng, dims, jnp.float32)
    if split:
        drawn = drawn * steps_of(rng, dims, split, -0.22, 0.18)
    return jnp.clip(drawn, -limit, limit).astype(kind)


def noise_with(stream_key, shape, scale, bound, pieces, heavy, held_as=jnp.bfloat16):
    drawn = scale * jax.random.normal(stream_key, shape, jnp.float32)
    if pieces:
        drawn = drawn * steps_of(stream_key, shape, pieces, -0.22, 0.18)
    return jnp.clip(raised(drawn, jax.random.fold_in(stream_key, 3), *heavy), -bound, bound).astype(held_as)


def setup_inputs(seed: int = 0) -> dict:
    arg_keys = jax.random.split(jax.random.key(seed), 8)
    queries = scatter_about(arg_keys[0], (SEQ, D), 1.0, 6.0, ((0, 64), (1, 16)))
    keys = scatter_about(arg_keys[1], (SEQ, D), 1.0, 6.0, ((0, 64), (1, 16)))
    values = scatter_about(arg_keys[2], (SEQ, D), 1.0, 6.0, ((0, 64), (1, 16)))
    short_taps = scatter_about(arg_keys[3], (3, SHORT, D), SHORT ** -0.5, 3.5, ((2, 16),), jnp.float32)
    long_rates = jnp.clip(jnp.exp(math.log(0.05) - 9.927204 * jax.random.uniform(arg_keys[4], (D, MODES), jnp.float32) ** steps_of(arg_keys[4], (D, MODES), ((0, 16),), -0.2, 0.2)), 2.441406195430318e-06, 0.05)
    long_resid = scatter_about(arg_keys[5], (D, MODES), 0.25, 1.5, ((0, 16),), jnp.float32)
    out_weight = noise_with(arg_keys[6], (D, OUT), D ** -0.5, 0.09375, ((0, 16),), (0, 1, 16, 2.0))
    return {"queries": queries, "keys": keys, "values": values, "short_taps": short_taps, "long_rates": long_rates, "long_resid": long_resid, "out_weight": out_weight}


def short_filter(stream, filter_taps):
    tail_len = filter_taps.shape[0] - 1
    length = stream.shape[0]
    leading = jnp.zeros((tail_len, stream.shape[1]), stream.dtype)
    extended = jnp.concatenate([leading, stream], axis=0).astype(jnp.float32)
    accum_sum = jnp.zeros(stream.shape, jnp.float32)
    for tap_index in range(filter_taps.shape[0]):
        accum_sum = accum_sum + filter_taps[tap_index] * extended[tail_len - tap_index:tail_len - tap_index + length]
    return accum_sum

def long_filter(product, long_rates, long_resid):
    decay = jnp.exp(-long_rates)
    coeff = long_resid * jnp.sqrt(-jnp.expm1(-2.0 * long_rates))

    def advance(carry_state, row_in):
        carry_state = decay * carry_state + row_in.astype(jnp.float32)[:, None]
        return (carry_state, lax.optimization_barrier(jnp.sum(coeff * carry_state, axis=1)))
    start_state = jnp.zeros(long_rates.shape, jnp.float32)
    _, result = lax.scan(advance, start_state, product)
    return result

def reference(queries, keys, values, short_taps, long_rates, long_resid, out_weight):
    q_feat = short_filter(queries, short_taps[0])
    k_feat = short_filter(keys, short_taps[1])
    v_feat = short_filter(values, short_taps[2])
    product = (k_feat * v_feat).astype(jnp.bfloat16)
    long_out = long_filter(product, long_rates, long_resid).astype(jnp.bfloat16)
    long_out = lax.optimization_barrier(long_out)
    gated = (q_feat * long_out.astype(jnp.float32)).astype(jnp.bfloat16)
    return jnp.dot(gated, out_weight, preferred_element_type=jnp.float32).astype(jnp.bfloat16)
```

```python
import jax
import jax.numpy as jnp
from jax import lax
from jax.experimental import pallas as pl
from jax.experimental.pallas import tpu as pltpu
from jax.sharding import PartitionSpec as P

MESH = pl.DeviceIdType.MESH
F32 = jnp.float32
BF16 = jnp.bfloat16
RUN = 8
BLOCK = 16
LANES = 128


def one_minus_exp(u):
    series = jnp.ones_like(u)
    for n in range(8, 1, -1):
        series = 1.0 - u * (1.0 / n) * series
    return jnp.where(u < 0.125, u * series, 1.0 - jnp.exp(-u))


def kernel(
    q_hbm, k_hbm, v_hbm, taps_hbm, rate_hbm, resid_hbm, w_hbm, o_ref,
    q_in, k_in, v_in, taps, rate_in, resid_in, w_own, w_par,
    q_ext, k_ext, v_ext, p_ext, p_group, halo_out, halo_in,
    rate, decay, coeff, heads, prefix, span, response, decay_b, gain_b, starts, local, q_feat,
    z_out, z_in, y_out, y_in, g_own, g_par, x_out, x_in, x_keep, h_out, h_in, unperm,
    in_sem, w_sem, wp_send, wp_recv, halo_sem, z_send, z_recv, y_send, y_recv, g_send, g_recv,
    x_send, x_recv, h_send, h_recv,
):
    rows, channels = q_in.shape
    rows_y, xs = y_in.shape[0] + 1, x_in.shape[1] + 1
    chunks, chunk = x_out.shape[0], x_out.shape[2]
    cols = h_out.shape[2]
    per = rows // BLOCK
    ctx, tp = lax.axis_index("ctx"), lax.axis_index("tp")
    y, z = ctx // RUN, ctx % RUN
    x, half, core = tp // 4, (tp // 2) % 2, tp % 2
    n_ctx = rows_y * RUN
    groups = [slice(g * LANES, (g + 1) * LANES) for g in range(channels // LANES)]

    def put(src, dst, send, recv, device):
        return pltpu.make_async_remote_copy(
            src_ref=src, dst_ref=dst, send_sem=send, recv_sem=recv, device_id=device, device_id_type=MESH
        )

    along_z = [(y * RUN + (z + d) % RUN, tp) for d in range(1, RUN)]
    along_y = [(((y + d) % rows_y) * RUN + z, tp) for d in range(1, rows_y)]
    along_x = [(ctx, ((x + d) % xs) * 4 + half * 2 + core) for d in range(1, xs)]
    other_core = (ctx, x * 4 + half * 2 + (1 - core))
    other_half = (ctx, x * 4 + (1 - half) * 2 + core)
    after, before = ((ctx + 1) % n_ctx, tp), ((ctx + n_ctx - 1) % n_ctx, tp)
    peers = along_z + along_y + along_x + [other_core, other_half, after, before]

    barrier = pltpu.get_barrier_semaphore()
    for peer in peers:
        pl.semaphore_signal(barrier, inc=1, device_id=peer, device_id_type=MESH)

    loads = [
        pltpu.make_async_copy(src, dst, in_sem.at[i])
        for i, (src, dst) in enumerate(
            [(q_hbm, q_in), (k_hbm, k_in), (v_hbm, v_in), (taps_hbm, taps), (rate_hbm, rate_in), (resid_hbm, resid_in)]
        )
    ]
    for load in loads:
        load.start()
    blocks = 2 * xs
    w_loads = [
        pltpu.make_async_copy(
            w_hbm.at[:, pl.ds(pl.multiple_of(b * 2 * cols + core * cols, cols), cols)], w_own.at[b], w_sem.at[b]
        )
        for b in range(blocks)
    ]
    w_shares = [
        put(
            w_hbm.at[:, pl.ds(pl.multiple_of(b * 2 * cols + (1 - core) * cols, cols), cols)],
            w_par.at[b], wp_send.at[b], wp_recv.at[b], other_core,
        )
        for b in range(blocks)
    ]

    for load in loads:
        load.wait()
    halo_out[...] = jnp.zeros((8, channels), F32)
    for s, stream in enumerate([q_in, k_in, v_in]):
        last = stream[rows - 16 :, :].astype(F32)
        halo_out[2 * s : 2 * s + 2, :] = last[14:16]
    for ext in (k_ext, v_ext):
        ext[0:8, :] = jnp.zeros((8, channels), F32)
    pl.semaphore_wait(barrier, len(peers))
    halo = put(halo_out, halo_in, halo_sem.at[0], halo_sem.at[1], after)
    halo.start()
    for w_load in w_loads:
        w_load.start()

    for stream, ext in [(k_in, k_ext), (v_in, v_ext)]:
        for a in range(0, rows, 16):
            ext[8 + a : 24 + a, :] = stream[a : a + 16, :].astype(F32)

    def feature(ext, n, first, count):
        total = taps[n, 0:1, :] * ext[8 + first : 8 + first + count, :]
        total = total + taps[n, 1:2, :] * ext[7 + first : 7 + first + count, :]
        return total + taps[n, 2:3, :] * ext[6 + first : 6 + first + count, :]

    def product(first, count):
        value = feature(k_ext, 1, first, count) * feature(v_ext, 2, first, count)
        return value.astype(BF16).astype(F32)

    row_index = lax.broadcasted_iota(jnp.int32, (8, channels), 0)
    p_ext[0:8, :] = jnp.where(row_index < 2, 0.0, product(0, 8))
    for a in range(8, rows, 8):
        p_ext[a : a + 8, :] = product(a, 8)

    rate[...] = rate_in[...]
    decay[...] = jnp.exp(-rate[...])
    coeff[...] = resid_in[...] * jnp.sqrt(one_minus_exp(2.0 * rate[...]))

    step = decay[...]
    low, high = jnp.zeros_like(step), jnp.zeros_like(step)
    for t in range(rows // 2):
        if t % BLOCK == 0:
            prefix[t // BLOCK] = low
            prefix[(t + rows // 2) // BLOCK] = high
        low = step * low + p_ext[t : t + 1, :]
        high = step * high + p_ext[t + rows // 2 : t + rows // 2 + 1, :]
    middle, modes = low, step.shape[0]
    own = high + jnp.exp(rate[...] * (-0.5 * rows)) * middle
    head_gain = jnp.exp(rate[...] * (2.0 - rows))
    whole = jnp.exp(rate[...] * (-1.0 * rows))

    halo.wait()
    inside = jnp.where(ctx > 0, halo_in[...], 0.0)
    k_ext[6:8, :] = inside[2:4, :]
    v_ext[6:8, :] = inside[4:6, :]
    p_ext[0:8, :] = product(0, 8)
    heads[...] = step * p_ext[0:1, :] + p_ext[1:2, :]
    own = own + head_gain * heads[...]

    z_out[...] = own.astype(BF16)
    z_copies = [put(z_out, z_in.at[d - 1], z_send.at[d - 1], z_recv.at[d - 1], along_z[d - 1]) for d in range(1, RUN)]
    for copy in z_copies:
        copy.start()
    for w_share in w_shares:
        w_share.start()

    for b in range(1, per):
        span[b] = jnp.exp(rate[...] * (2.0 - BLOCK * b))
        if b > per // 2:
            prefix[b] = prefix[b] + jnp.exp(rate[...] * (1.0 * (per // 2 - b) * BLOCK)) * middle
    prefix[per // 2] = middle
    term = coeff[...]
    for k in range(BLOCK):
        response[k : k + 1, :] = jnp.sum(term, axis=0, keepdims=True)
        term = term * step
    first_gain = coeff[...] * step
    for g, lanes in enumerate(groups):
        for b in range(per):
            decay_b[g, pl.ds(b, modes, stride=per), :] = step[:, lanes]
            gain_b[g, pl.ds(b, modes, stride=per), :] = first_gain[:, lanes]
        q_ext[g, 6:8, :] = inside[0:2, lanes]
        for a in range(0, rows, 16):
            q_ext[g, 8 + a : 24 + a, :] = q_in[a : a + 16, lanes].astype(F32)
            p_group[g, a : a + 16, :] = p_ext[a : a + 16, lanes]
        for r in range(BLOCK):
            total = taps[0, 0:1, lanes] * q_ext[g, pl.ds(8 + r, per, stride=BLOCK), :]
            total = total + taps[0, 1:2, lanes] * q_ext[g, pl.ds(7 + r, per, stride=BLOCK), :]
            total = total + taps[0, 2:3, lanes] * q_ext[g, pl.ds(6 + r, per, stride=BLOCK), :]
            q_feat[r * per : (r + 1) * per, lanes] = total

    def convolve(group, carry):
        lanes = pl.ds(pl.multiple_of(group * LANES, LANES), LANES)
        inputs = [p_group[group, pl.ds(r, per, stride=BLOCK), :] for r in range(BLOCK)]
        for r in range(BLOCK):
            total = response[0:1, lanes] * inputs[r]
            for k in range(1, r + 1):
                total = total + response[k : k + 1, lanes] * inputs[r - k]
            local[r * per : (r + 1) * per, lanes] = total
        return carry

    lax.fori_loop(0, channels // LANES, convolve, 0)

    for copy in z_copies:
        copy.wait()
    before_me = jnp.zeros_like(step)
    for d in range(RUN - 1, 0, -1):
        before_me = whole * before_me + jnp.where(d <= z, z_in[d - 1].astype(F32), 0.0)
    total = whole * before_me + own
    for d in range(RUN - 1, 0, -1):
        total = jnp.where(d > z, whole * total + z_in[d - 1].astype(F32), total)

    y_out[...] = total.astype(BF16)
    y_copies = [
        put(y_out, y_in.at[d - 1], y_send.at[d - 1], y_recv.at[d - 1], along_y[d - 1]) for d in range(1, rows_y)
    ]
    for copy in y_copies:
        copy.start()
    row_decay = jnp.exp(rate[...] * (-1.0 * rows * RUN))
    my_decay = jnp.exp(rate[...] * (-1.0 * rows * z.astype(F32)))
    for w_load in w_loads:
        w_load.wait()
    for w_share in w_shares:
        w_share.wait()
    for copy in y_copies:
        copy.wait()
    arriving = jnp.zeros_like(step)
    for d in range(rows_y - 1, 0, -1):
        arriving = row_decay * arriving + jnp.where(d <= y, y_in[d - 1].astype(F32), 0.0)
    state = before_me + my_decay * arriving
    second = step * step * state + heads[...]
    for b in range(per):
        if b > 0:
            state = prefix[b] + span[b] * second
        for g, lanes in enumerate(groups):
            starts[g, pl.ds(b, modes, stride=per), :] = state[:, lanes]

    steps = BLOCK // chunks
    g_copies, x_copies, h_copies = [], [], []
    for c in range(chunks):

        def gate(group, carry):
            lanes = pl.ds(pl.multiple_of(group * LANES, LANES), LANES)
            shape = (modes, per, LANES)
            ratio = decay_b[group].reshape(shape)
            term = starts[group].reshape(shape)
            if c == 0:
                term = term * gain_b[group].reshape(shape)
            for r in range(c * steps, (c + 1) * steps, 2):
                pair = []
                for one in (r, r + 1):
                    here = slice(one * per, (one + 1) * per)
                    value = local[here, lanes] + jnp.sum(term, axis=0)
                    term = term * ratio
                    pair.append(q_feat[here, lanes] * value.astype(BF16).astype(F32))
                g_own[r * per : (r + 2) * per, lanes] = jnp.concatenate(pair, axis=0).astype(BF16)
            if c + 1 < chunks:
                starts[group] = term.reshape(modes * per, LANES)
            return carry

        lax.fori_loop(0, channels // LANES, gate, 0)
        piece = pl.ds(c * chunk, chunk)
        copy = put(g_own.at[piece], g_par.at[piece], g_send.at[c], g_recv.at[c], other_core)
        copy.start()
        g_copies.append(copy)

    for c in range(chunks):
        g_copies[c].wait()
        here = slice(c * chunk, (c + 1) * chunk)
        mine, theirs = g_own[here, :], g_par[here, :]

        def share(b):
            return jnp.dot(mine, w_own[b], preferred_element_type=F32) + jnp.dot(
                theirs, w_par[b], preferred_element_type=F32
            )

        for d in (2, 1, 3):
            to = (x + d) % xs
            for h in range(2):
                x_out[c, d - 1, :, h * cols : (h + 1) * cols] = share(to * 2 + h).astype(BF16)
            copy = put(x_out.at[c, d - 1], x_in.at[c, d - 1], x_send.at[c, d - 1], x_recv.at[c, d - 1], along_x[d - 1])
            copy.start()
            x_copies.append(copy)
        for h in range(2):
            x_keep[c, h] = share(x * 2 + h)

    for c in range(chunks):
        for copy in x_copies[c * (xs - 1) : (c + 1) * (xs - 1)]:
            copy.wait()
        for h in range(2):
            for a in range(0, chunk, 16):
                value = x_keep[c, h, a : a + 16, :]
                for d in range(1, xs):
                    value = value + x_in[c, d - 1, a : a + 16, h * cols : (h + 1) * cols].astype(F32)
                x_keep[c, h, a : a + 16, :] = value
        h_out[c] = x_keep[c, 1 - half].astype(BF16)
        copy = put(h_out.at[c], h_in.at[c], h_send.at[c], h_recv.at[c], other_half)
        copy.start()
        h_copies.append(copy)

    for c in range(chunks):
        h_copies[c].wait()
        for a in range(0, chunk, 16):
            value = x_keep[c, half, a : a + 16, :] + h_in[c, a : a + 16, :].astype(F32)
            r = (c * chunk + a) // per
            for i in range(16 // per):
                for g in range(cols // LANES):
                    part = value[i * per : (i + 1) * per, g * LANES : (g + 1) * LANES]
                    unperm[g, pl.ds(r + i, per, stride=BLOCK), :] = part
    for g in range(cols // LANES):
        o_ref[:, g * LANES : (g + 1) * LANES] = unperm[g].astype(BF16)


def solution(mesh):
    n_ctx, n_tp = mesh.shape["ctx"], mesh.shape["tp"]
    rows_y, xs = n_ctx // RUN, n_tp // 4
    chunks = 2

    def shards(queries, keys, values, short_taps, long_rates, long_resid, out_weight):
        rows, channels = queries.shape
        modes = long_rates.shape[1]
        out = out_weight.shape[1]
        cols = out // n_tp
        chunk = rows // chunks
        state = (modes, channels)
        stream = pltpu.VMEM((rows, channels), BF16)
        sem = pltpu.SemaphoreType.DMA
        return pl.pallas_call(
            kernel,
            name="hyena",
            out_shape=jax.ShapeDtypeStruct((rows, cols), BF16),
            in_specs=[pl.BlockSpec(memory_space=pltpu.HBM)] * 7,
            out_specs=pl.BlockSpec(memory_space=pltpu.VMEM),
            scratch_shapes=[
                stream, stream, stream,
                pltpu.VMEM(short_taps.shape, F32),
                pltpu.VMEM(state, F32),
                pltpu.VMEM(state, F32),
                pltpu.VMEM((2 * xs, channels, cols), BF16),
                pltpu.VMEM((2 * xs, channels, cols), BF16),
                pltpu.VMEM((channels // LANES, rows + 8, LANES), F32),
                pltpu.VMEM((rows + 8, channels), F32),
                pltpu.VMEM((rows + 8, channels), F32),
                pltpu.VMEM((rows, channels), F32),
                pltpu.VMEM((channels // LANES, rows, LANES), F32),
                pltpu.VMEM((8, channels), F32),
                pltpu.VMEM((8, channels), F32),
                pltpu.VMEM(state, F32),
                pltpu.VMEM(state, F32),
                pltpu.VMEM(state, F32),
                pltpu.VMEM(state, F32),
                pltpu.VMEM((rows // BLOCK,) + state, F32),
                pltpu.VMEM((rows // BLOCK,) + state, F32),
                pltpu.VMEM((BLOCK, channels), F32),
                pltpu.VMEM((channels // LANES, modes * (rows // BLOCK), LANES), F32),
                pltpu.VMEM((channels // LANES, modes * (rows // BLOCK), LANES), F32),
                pltpu.VMEM((channels // LANES, modes * (rows // BLOCK), LANES), F32),
                pltpu.VMEM((rows, channels), F32),
                pltpu.VMEM((rows, channels), F32),
                pltpu.VMEM(state, BF16),
                pltpu.VMEM((RUN - 1,) + state, BF16),
                pltpu.VMEM(state, BF16),
                pltpu.VMEM((rows_y - 1,) + state, BF16),
                stream, stream,
                pltpu.VMEM((chunks, xs - 1, chunk, 2 * cols), BF16),
                pltpu.VMEM((chunks, xs - 1, chunk, 2 * cols), BF16),
                pltpu.VMEM((chunks, 2, chunk, cols), F32),
                pltpu.VMEM((chunks, chunk, cols), BF16),
                pltpu.VMEM((chunks, chunk, cols), BF16),
                pltpu.VMEM((cols // LANES, rows, LANES), F32),
                sem((6,)),
                sem((2 * xs,)), sem((2 * xs,)), sem((2 * xs,)),
                sem((2,)),
                sem((RUN - 1,)), sem((RUN - 1,)),
                sem((rows_y - 1,)), sem((rows_y - 1,)),
                sem((chunks,)), sem((chunks,)),
                sem((chunks, xs - 1)), sem((chunks, xs - 1)),
                sem((chunks,)), sem((chunks,)),
            ],
            compiler_params=pltpu.CompilerParams(
                collective_id=0, has_side_effects=True, vmem_limit_bytes=62 * 1024 * 1024
            ),
        )(queries, keys, values, short_taps, long_rates.T, long_resid.T, out_weight)

    return jax.shard_map(
        shards,
        mesh=mesh,
        in_specs=(
            P("ctx", "tp"),
            P("ctx", "tp"),
            P("ctx", "tp"),
            P(None, None, "tp"),
            P("tp", None),
            P("tp", None),
            P("tp", None),
        ),
        out_specs=P("ctx", "tp"),
        check_vma=False,
    )
```

```python
import jax
import jax.numpy as jnp
from jax import lax
from jax.experimental import pallas as pl
from jax.experimental.pallas import tpu as pltpu
from jax.sharding import PartitionSpec as P

MESH = pl.DeviceIdType.MESH
F32 = jnp.float32
BF16 = jnp.bfloat16
RUN = 8
BLOCK = 16
LANES = 128


def one_minus_exp(u):
    series = jnp.ones_like(u)
    for n in range(8, 1, -1):
        series = 1.0 - u * (1.0 / n) * series
    return jnp.where(u < 0.125, u * series, 1.0 - jnp.exp(-u))


def packed(parts):
    value = jnp.concatenate(parts, axis=0)
    width = value.shape[1] // 2
    return jnp.concatenate([value[:, :width], value[:, width:]], axis=0).astype(BF16)


def unpacked(block):
    value = block.astype(F32)
    return jnp.concatenate([value[0:8], value[8:16]], axis=1)


def kernel(
    q_hbm, k_hbm, v_hbm, taps_hbm, rate_hbm, resid_hbm, w_hbm, o_ref,
    q_in, k_in, v_in, taps, rate_in, resid_in, w_own, w_par,
    q_ext, k_ext, v_ext, p_ext, p_group, halo_out, halo_in,
    rate, decay, coeff, heads, prefix, span, response, decay_b, gain_b, starts, local, q_feat,
    z_out, z_in, y_out, y_in, g_own, g_par, x_out, x_in, x_keep, h_out, h_in, unperm,
    in_sem, w_sem, wp_send, wp_recv, halo_sem, z_send, z_recv, y_send, y_recv, g_send, g_recv,
    x_send, x_recv, h_send, h_recv, ring_sem,
):
    rows, channels = q_in.shape
    rows_y, xs = y_in.shape[0], x_in.shape[2] + 1
    chunks, chunk = h_out.shape[0], h_out.shape[1]
    cols = h_out.shape[2]
    per = rows // BLOCK
    ctx, tp = lax.axis_index("ctx"), lax.axis_index("tp")
    y, z = ctx // RUN, ctx % RUN
    x, half, core = tp // 4, (tp // 2) % 2, tp % 2
    n_ctx = rows_y * RUN
    groups = [slice(g * LANES, (g + 1) * LANES) for g in range(channels // LANES)]

    def put(src, dst, send, recv, device):
        return pltpu.make_async_remote_copy(
            src_ref=src, dst_ref=dst, send_sem=send, recv_sem=recv, device_id=device, device_id_type=MESH
        )

    along_z = [(y * RUN + (z + d) % RUN, tp) for d in range(1, RUN)]
    along_y = [(((y + d) % rows_y) * RUN + z, tp) for d in range(1, rows_y)]
    along_x = [(ctx, ((x + d) % xs) * 4 + half * 2 + core) for d in range(1, xs)]
    other_core = (ctx, x * 4 + half * 2 + (1 - core))
    other_half = (ctx, x * 4 + (1 - half) * 2 + core)
    after, before = ((ctx + 1) % n_ctx, tp), ((ctx + n_ctx - 1) % n_ctx, tp)

    far_mate = (y * RUN + (z + RUN // 2) % RUN, other_half[1])
    near_y = [d for d in range(1, rows_y) if min(d, rows_y - d) <= 2]
    hop_y = [d for d in range(1, rows_y) if min(d, rows_y - d) == 2]
    told = along_z + along_x + [other_core, before, far_mate] + [along_y[d - 1] for d in near_y]

    barrier = pltpu.get_barrier_semaphore()
    for peer in told:
        pl.semaphore_signal(barrier, inc=1, device_id=peer, device_id_type=MESH)

    loads = [
        pltpu.make_async_copy(src, dst, in_sem.at[i])
        for i, (src, dst) in enumerate(
            [(q_hbm, q_in), (k_hbm, k_in), (v_hbm, v_in), (taps_hbm, taps), (rate_hbm, rate_in), (resid_hbm, resid_in)]
        )
    ]
    for load in loads:
        load.start()
    blocks = 2 * xs
    w_loads = [
        pltpu.make_async_copy(
            w_hbm.at[:, pl.ds(pl.multiple_of(b * 2 * cols + core * cols, cols), cols)], w_own.at[b], w_sem.at[b]
        )
        for b in range(blocks)
    ]
    w_shares = [
        put(
            w_hbm.at[:, pl.ds(pl.multiple_of(b * 2 * cols + (1 - core) * cols, cols), cols)],
            w_par.at[b], wp_send.at[b], wp_recv.at[b], other_core,
        )
        for b in range(blocks)
    ]

    for load in loads:
        load.wait()
    for w_load in w_loads:
        w_load.start()
    for ext in (k_ext, v_ext):
        ext[0:8, :] = jnp.zeros((8, channels), F32)

    for stream, ext in [(k_in, k_ext), (v_in, v_ext)]:
        for a in range(0, rows, 16):
            ext[8 + a : 24 + a, :] = stream[a : a + 16, :].astype(F32)

    def feature(ext, n, first, count):
        total = taps[n, 0:1, :] * ext[8 + first : 8 + first + count, :]
        total = total + taps[n, 1:2, :] * ext[7 + first : 7 + first + count, :]
        return total + taps[n, 2:3, :] * ext[6 + first : 6 + first + count, :]

    def product(first, count):
        value = feature(k_ext, 1, first, count) * feature(v_ext, 2, first, count)
        return value.astype(BF16).astype(F32)

    row_index = lax.broadcasted_iota(jnp.int32, (8, channels), 0)
    p_ext[0:8, :] = jnp.where(row_index < 2, 0.0, product(0, 8))
    for a in range(8, rows, 8):
        p_ext[a : a + 8, :] = product(a, 8)

    rate[...] = rate_in[...]
    decay[...] = jnp.exp(-rate[...])
    coeff[...] = resid_in[...] * jnp.sqrt(one_minus_exp(2.0 * rate[...]))

    step = decay[...]
    low, high = jnp.zeros_like(step), jnp.zeros_like(step)
    for t in range(rows // 2):
        if t % BLOCK == 0:
            prefix[t // BLOCK] = low
            prefix[(t + rows // 2) // BLOCK] = high
        low = step * low + p_ext[t : t + 1, :]
        high = step * high + p_ext[t + rows // 2 : t + rows // 2 + 1, :]
    middle, modes = low, step.shape[0]
    own = high + jnp.exp(rate[...] * (-0.5 * rows)) * middle
    head_gain = jnp.exp(rate[...] * (2.0 - rows))
    whole = jnp.exp(rate[...] * (-1.0 * rows))

    k_first, v_first = k_in[0:16, :].astype(F32), v_in[0:16, :].astype(F32)
    q_last, k_last, v_last = (stream[rows - 16 :, :].astype(F32)[14:16] for stream in (q_in, k_in, v_in))
    z_out[:, :channels] = own.astype(BF16)
    z_out[:, channels:] = packed([k_first[0:2], v_first[0:2], k_last, v_last])
    z_in[z] = z_out[...]
    halo_out[...] = packed([q_last, k_last, v_last, jnp.zeros_like(v_last)])
    pl.semaphore_wait(barrier, len(told))
    z_copies = [put(z_out, z_in.at[z], z_send.at[d - 1], z_recv.at[z], along_z[d - 1]) for d in range(1, RUN)]
    for copy in z_copies:
        copy.start()
    for d in hop_y:
        pl.semaphore_signal(ring_sem, inc=1, device_id=along_y[d - 1], device_id_type=MESH)
    halo = put(halo_out, halo_in, halo_sem.at[0], halo_sem.at[1], after)
    halo.start()
    for w_share in w_shares:
        w_share.start()

    halo.wait()
    inside = jnp.where(ctx > 0, unpacked(halo_in[...]), 0.0)
    k_ext[6:8, :] = inside[2:4, :]
    v_ext[6:8, :] = inside[4:6, :]
    p_ext[0:8, :] = product(0, 8)
    heads[...] = step * p_ext[0:1, :] + p_ext[1:2, :]

    def boundary(last, first):
        value = [1.0, 1.0]
        for n, old, new in ((1, 4, 0), (2, 6, 2)):
            tap = [taps[n, j : j + 1, :] for j in range(3)]
            line = [last[old : old + 1], last[old + 1 : old + 2], first[new : new + 1], first[new + 1 : new + 2]]
            for i in range(2):
                value[i] = value[i] * (tap[0] * line[i + 2] + tap[1] * line[i + 1] + tap[2] * line[i])
        value = [one.astype(BF16).astype(F32) for one in value]
        return step * value[0] + value[1]

    for b in range(1, per):
        span[b] = jnp.exp(rate[...] * (2.0 - BLOCK * b))
        if b > per // 2:
            prefix[b] = prefix[b] + jnp.exp(rate[...] * (1.0 * (per // 2 - b) * BLOCK)) * middle
    prefix[per // 2] = middle
    term = coeff[...]
    for k in range(BLOCK):
        response[k : k + 1, :] = jnp.sum(term, axis=0, keepdims=True)
        term = term * step
    first_gain = coeff[...] * step
    for g, lanes in enumerate(groups):
        for b in range(per):
            decay_b[g, pl.ds(b, modes, stride=per), :] = step[:, lanes]
            gain_b[g, pl.ds(b, modes, stride=per), :] = first_gain[:, lanes]
        q_ext[g, 6:8, :] = inside[0:2, lanes]
        for a in range(0, rows, 16):
            q_ext[g, 8 + a : 24 + a, :] = q_in[a : a + 16, lanes].astype(F32)
            p_group[g, a : a + 16, :] = p_ext[a : a + 16, lanes]
        for r in range(BLOCK):
            total = taps[0, 0:1, lanes] * q_ext[g, pl.ds(8 + r, per, stride=BLOCK), :]
            total = total + taps[0, 1:2, lanes] * q_ext[g, pl.ds(7 + r, per, stride=BLOCK), :]
            total = total + taps[0, 2:3, lanes] * q_ext[g, pl.ds(6 + r, per, stride=BLOCK), :]
            q_feat[r * per : (r + 1) * per, lanes] = total

    def convolve(group, carry):
        lanes = pl.ds(pl.multiple_of(group * LANES, LANES), LANES)
        inputs = [p_group[group, pl.ds(r, per, stride=BLOCK), :] for r in range(BLOCK)]
        for r in range(BLOCK):
            total = response[0:1, lanes] * inputs[r]
            for k in range(1, r + 1):
                total = total + response[k : k + 1, lanes] * inputs[r - k]
            local[r * per : (r + 1) * per, lanes] = total
        return carry

    lax.fori_loop(0, channels // LANES, convolve, 0)

    for d in range(1, RUN):
        z_copies[d - 1].wait_send()
        there = (z + d) % RUN
        put(z_out, z_in.at[there], z_send.at[d - 1], z_recv.at[there], along_z[d - 1]).wait_recv()
    before_me, total = jnp.zeros_like(step), jnp.zeros_like(step)
    edges = [unpacked(z_in[i, :, channels:]) for i in range(RUN)]
    for i in range(RUN):
        value = z_in[i, :, :channels].astype(F32)
        if i > 0:
            value = value + head_gain * boundary(edges[i - 1], edges[i])
        before_me = jnp.where(i < z, whole * before_me + value, before_me)
        total = whole * total + value

    y_out[:, :channels] = total.astype(BF16)
    row_edges = [edges[0][0:2], edges[0][2:4], edges[RUN - 1][4:6], edges[RUN - 1][6:8]]
    y_out[:, channels:] = packed(row_edges)
    y_in[y] = y_out[...]
    pl.semaphore_wait(ring_sem, len(hop_y))
    y_copies = [put(y_out, y_in.at[y], y_send.at[d - 1], y_recv.at[y], along_y[d - 1]) for d in range(1, rows_y)]
    for d in sorted(range(1, rows_y), key=lambda d: -min(d, rows_y - d)):
        pl.when(y + d < rows_y)(y_copies[d - 1].start)
    row_decay = jnp.exp(rate[...] * (-1.0 * rows * RUN))
    row_gain = jnp.exp(rate[...] * (2.0 - rows * RUN))
    my_gain = jnp.exp(rate[...] * (2.0 - rows * z.astype(F32)))
    for w_load in w_loads:
        w_load.wait()
    for w_share in w_shares:
        w_share.wait()
    for d in range(1, rows_y):
        pl.when(y + d < rows_y)(y_copies[d - 1].wait_send)
        there = (y + rows_y - d) % rows_y
        arrived = put(y_out, y_in.at[there], y_send.at[d - 1], y_recv.at[there], along_y[d - 1])
        pl.when(y >= d)(arrived.wait_recv)
    state = jnp.zeros_like(step)
    last = jnp.zeros((8, channels), F32)
    row_heads = jnp.zeros_like(step)
    for i in range(rows_y):
        edge = unpacked(y_in[i, :, channels:])
        head = boundary(last, edge)
        row_heads = jnp.where(i == y, head, row_heads)
        value = row_decay * state + row_gain * head + y_in[i, :, :channels].astype(F32)
        state = jnp.where(i < y, value, state)
        last = edge
    state = jnp.where(z > 0, before_me + my_gain * (step * step * state + row_heads), state)
    second = step * step * state + heads[...]
    for b in range(per):
        if b > 0:
            state = prefix[b] + span[b] * second
        for g, lanes in enumerate(groups):
            starts[g, pl.ds(b, modes, stride=per), :] = state[:, lanes]

    steps = BLOCK // chunks
    g_copies, x_copies, h_copies = [], [], []
    for c in range(chunks):

        def gate(group, carry):
            lanes = pl.ds(pl.multiple_of(group * LANES, LANES), LANES)
            shape = (modes, per, LANES)
            ratio = decay_b[group].reshape(shape)
            term = starts[group].reshape(shape)
            if c == 0:
                term = term * gain_b[group].reshape(shape)
            for r in range(c * steps, (c + 1) * steps, 2):
                pair = []
                for one in (r, r + 1):
                    here = slice(one * per, (one + 1) * per)
                    value = local[here, lanes] + jnp.sum(term, axis=0)
                    term = term * ratio
                    pair.append(q_feat[here, lanes] * value.astype(BF16).astype(F32))
                g_own[r * per : (r + 2) * per, lanes] = jnp.concatenate(pair, axis=0).astype(BF16)
            if c + 1 < chunks:
                starts[group] = term.reshape(modes * per, LANES)
            return carry

        lax.fori_loop(0, channels // LANES, gate, 0)
        piece = pl.ds(c * chunk, chunk)
        copy = put(g_own.at[piece], g_par.at[piece], g_send.at[c], g_recv.at[c], other_core)
        copy.start()
        g_copies.append(copy)

    def share(c, b):
        here = slice(c * chunk, (c + 1) * chunk)
        value = jnp.dot(g_own[here, :], w_own[b], preferred_element_type=F32)
        return value + jnp.dot(g_par[here, :], w_par[b], preferred_element_type=F32)

    for part, h in enumerate((1 - half, half)):
        for c in range(chunks):
            if part == 0:
                g_copies[c].wait()
            for d in (2, 1, 3):
                to = (x + d) % xs
                x_out[part, c, d - 1] = share(c, to * 2 + h).astype(BF16)
                copy = put(
                    x_out.at[part, c, d - 1], x_in.at[part, c, d - 1],
                    x_send.at[part, c, d - 1], x_recv.at[part, c, d - 1], along_x[d - 1],
                )
                copy.start()
                x_copies.append(copy)
    for part, h in enumerate((1 - half, half)):
        for c in range(chunks):
            x_keep[part, c] = share(c, x * 2 + h)

    for part in range(2):
        for c in range(chunks):
            for copy in x_copies[: xs - 1]:
                copy.wait()
            x_copies = x_copies[xs - 1 :]
            for a in range(0, chunk, 16):
                value = x_keep[part, c, a : a + 16, :]
                for d in range(1, xs):
                    value = value + x_in[part, c, d - 1, a : a + 16, :].astype(F32)
                if part == 0:
                    h_out[c, a : a + 16, :] = value.astype(BF16)
                else:
                    x_keep[part, c, a : a + 16, :] = value
            if part == 0:
                copy = put(h_out.at[c], h_in.at[c], h_send.at[c], h_recv.at[c], other_half)
                copy.start()
                h_copies.append(copy)

    for c in range(chunks):
        h_copies[c].wait()
        for a in range(0, chunk, 16):
            value = x_keep[1, c, a : a + 16, :] + h_in[c, a : a + 16, :].astype(F32)
            r = (c * chunk + a) // per
            for i in range(16 // per):
                for g in range(cols // LANES):
                    part = value[i * per : (i + 1) * per, g * LANES : (g + 1) * LANES]
                    unperm[g, pl.ds(r + i, per, stride=BLOCK), :] = part
    for g in range(cols // LANES):
        o_ref[:, g * LANES : (g + 1) * LANES] = unperm[g].astype(BF16)


def solution(mesh):
    n_ctx, n_tp = mesh.shape["ctx"], mesh.shape["tp"]
    rows_y, xs = n_ctx // RUN, n_tp // 4
    chunks = 2

    def shards(queries, keys, values, short_taps, long_rates, long_resid, out_weight):
        rows, channels = queries.shape
        modes = long_rates.shape[1]
        out = out_weight.shape[1]
        cols = out // n_tp
        chunk = rows // chunks
        state = (modes, channels)
        message = (modes, channels + channels // 2)
        stream = pltpu.VMEM((rows, channels), BF16)
        sem = pltpu.SemaphoreType.DMA
        return pl.pallas_call(
            kernel,
            name="hyena",
            out_shape=pltpu.VMEM((rows, cols), BF16),
            in_specs=[pl.BlockSpec(memory_space=pltpu.HBM)] * 7,
            out_specs=pl.BlockSpec(memory_space=pltpu.VMEM),
            scratch_shapes=[
                stream, stream, stream,
                pltpu.VMEM(short_taps.shape, F32),
                pltpu.VMEM(state, F32),
                pltpu.VMEM(state, F32),
                pltpu.VMEM((2 * xs, channels, cols), BF16),
                pltpu.VMEM((2 * xs, channels, cols), BF16),
                pltpu.VMEM((channels // LANES, rows + 8, LANES), F32),
                pltpu.VMEM((rows + 8, channels), F32),
                pltpu.VMEM((rows + 8, channels), F32),
                pltpu.VMEM((rows, channels), F32),
                pltpu.VMEM((channels // LANES, rows, LANES), F32),
                pltpu.VMEM((16, channels // 2), BF16),
                pltpu.VMEM((16, channels // 2), BF16),
                pltpu.VMEM(state, F32),
                pltpu.VMEM(state, F32),
                pltpu.VMEM(state, F32),
                pltpu.VMEM(state, F32),
                pltpu.VMEM((rows // BLOCK,) + state, F32),
                pltpu.VMEM((rows // BLOCK,) + state, F32),
                pltpu.VMEM((BLOCK, channels), F32),
                pltpu.VMEM((channels // LANES, modes * (rows // BLOCK), LANES), F32),
                pltpu.VMEM((channels // LANES, modes * (rows // BLOCK), LANES), F32),
                pltpu.VMEM((channels // LANES, modes * (rows // BLOCK), LANES), F32),
                pltpu.VMEM((rows, channels), F32),
                pltpu.VMEM((rows, channels), F32),
                pltpu.VMEM(message, BF16),
                pltpu.VMEM((RUN,) + message, BF16),
                pltpu.VMEM(message, BF16),
                pltpu.VMEM((rows_y,) + message, BF16),
                stream, stream,
                pltpu.VMEM((2, chunks, xs - 1, chunk, cols), BF16),
                pltpu.VMEM((2, chunks, xs - 1, chunk, cols), BF16),
                pltpu.VMEM((2, chunks, chunk, cols), F32),
                pltpu.VMEM((chunks, chunk, cols), BF16),
                pltpu.VMEM((chunks, chunk, cols), BF16),
                pltpu.VMEM((cols // LANES, rows, LANES), F32),
                sem((6,)),
                sem((2 * xs,)), sem((2 * xs,)), sem((2 * xs,)),
                sem((2,)),
                sem((RUN - 1,)), sem((RUN,)),
                sem((rows_y - 1,)), sem((rows_y,)),
                sem((chunks,)), sem((chunks,)),
                sem((2, chunks, xs - 1)), sem((2, chunks, xs - 1)),
                sem((chunks,)), sem((chunks,)),
                pltpu.SemaphoreType.REGULAR,
            ],
            compiler_params=pltpu.CompilerParams(
                collective_id=0, has_side_effects=True, vmem_limit_bytes=62 * 1024 * 1024
            ),
        )(queries, keys, values, short_taps, long_rates.T, long_resid.T, out_weight)

    return jax.shard_map(
        shards,
        mesh=mesh,
        in_specs=(
            P("ctx", "tp"),
            P("ctx", "tp"),
            P("ctx", "tp"),
            P(None, None, "tp"),
            P("tp", None),
            P("tp", None),
            P("tp", None),
        ),
        out_specs=P("ctx", "tp"),
        check_vma=False,
    )
```

```python
import jax
import jax.numpy as jnp
from jax import lax
from jax.experimental import pallas as pl
from jax.experimental.pallas import tpu as pltpu
from jax.sharding import PartitionSpec as P

MESH = pl.DeviceIdType.MESH
F32 = jnp.float32
BF16 = jnp.bfloat16
RUN = 8
BLOCK = 16
LANES = 128


def one_minus_exp(u):
    series = jnp.ones_like(u)
    for n in range(8, 1, -1):
        series = 1.0 - u * (1.0 / n) * series
    return jnp.where(u < 0.125, u * series, 1.0 - jnp.exp(-u))


def packed(parts):
    value = jnp.concatenate(parts, axis=0)
    width = value.shape[1] // 2
    return jnp.concatenate([value[:, :width], value[:, width:]], axis=0).astype(BF16)


def unpacked(block):
    value = block.astype(F32)
    return jnp.concatenate([value[0:8], value[8:16]], axis=1)


def kernel(
    q_hbm, k_hbm, v_hbm, taps_hbm, rate_hbm, resid_hbm, w_hbm, o_ref,
    q_in, k_in, v_in, taps, rate_in, resid_in, w_own, w_par,
    q_ext, k_ext, v_ext, p_ext, p_group, halo_out, halo_in,
    rate, decay, coeff, heads, prefix, span, response, decay_b, gain_b, starts, local, q_feat,
    z_out, z_in, y_out, y_in, g_own, g_par, x_out, x_in, x_keep, h_out, h_in, unperm,
    in_sem, w_sem, wp_send, wp_recv, halo_sem, z_send, z_recv, y_send, y_recv, g_send, g_recv,
    x_send, x_recv, h_send, h_recv, ring_sem,
):
    rows, channels = q_in.shape
    rows_y, xs = y_in.shape[0], x_in.shape[2] + 1
    chunks, chunk = h_out.shape[0], h_out.shape[1]
    cols = h_out.shape[2]
    per = rows // BLOCK
    ctx, tp = lax.axis_index("ctx"), lax.axis_index("tp")
    y, z = ctx // RUN, ctx % RUN
    x, half, core = tp // 4, (tp // 2) % 2, tp % 2
    n_ctx = rows_y * RUN
    groups = [slice(g * LANES, (g + 1) * LANES) for g in range(channels // LANES)]

    def put(src, dst, send, recv, device):
        return pltpu.make_async_remote_copy(
            src_ref=src, dst_ref=dst, send_sem=send, recv_sem=recv, device_id=device, device_id_type=MESH
        )

    along_z = [(y * RUN + (z + d) % RUN, tp) for d in range(1, RUN)]
    along_y = [(((y + d) % rows_y) * RUN + z, tp) for d in range(1, rows_y)]
    along_x = [(ctx, ((x + d) % xs) * 4 + half * 2 + core) for d in range(1, xs)]
    other_core = (ctx, x * 4 + half * 2 + (1 - core))
    other_half = (ctx, x * 4 + (1 - half) * 2 + core)
    after, before = ((ctx + 1) % n_ctx, tp), ((ctx + n_ctx - 1) % n_ctx, tp)

    far_mate = (y * RUN + (z + RUN // 2) % RUN, other_half[1])
    near_y = [d for d in range(1, rows_y) if min(d, rows_y - d) <= 2]
    hop_y = [d for d in range(1, rows_y) if min(d, rows_y - d) == 2]
    told = along_z + along_x + [other_core, before, far_mate] + [along_y[d - 1] for d in near_y]

    barrier = pltpu.get_barrier_semaphore()
    for peer in told:
        pl.semaphore_signal(barrier, inc=1, device_id=peer, device_id_type=MESH)

    loads = [
        pltpu.make_async_copy(src, dst, in_sem.at[i])
        for i, (src, dst) in enumerate(
            [(q_hbm, q_in), (k_hbm, k_in), (v_hbm, v_in), (taps_hbm, taps), (rate_hbm, rate_in), (resid_hbm, resid_in)]
        )
    ]
    for load in loads:
        load.start()
    blocks = 2 * xs
    w_loads = [
        pltpu.make_async_copy(
            w_hbm.at[:, pl.ds(pl.multiple_of(b * 2 * cols + core * cols, cols), cols)], w_own.at[b], w_sem.at[b]
        )
        for b in range(blocks)
    ]
    w_shares = [
        put(
            w_hbm.at[:, pl.ds(pl.multiple_of(b * 2 * cols + (1 - core) * cols, cols), cols)],
            w_par.at[b], wp_send.at[b], wp_recv.at[b], other_core,
        )
        for b in range(blocks)
    ]

    for load in loads:
        load.wait()
    for w_load in w_loads:
        w_load.start()
    for ext in (k_ext, v_ext):
        ext[0:8, :] = jnp.zeros((8, channels), F32)

    for stream, ext in [(k_in, k_ext), (v_in, v_ext)]:
        for a in range(0, rows, 16):
            ext[8 + a : 24 + a, :] = stream[a : a + 16, :].astype(F32)

    def feature(ext, n, first, count):
        total = taps[n, 0:1, :] * ext[8 + first : 8 + first + count, :]
        total = total + taps[n, 1:2, :] * ext[7 + first : 7 + first + count, :]
        return total + taps[n, 2:3, :] * ext[6 + first : 6 + first + count, :]

    def product(first, count):
        value = feature(k_ext, 1, first, count) * feature(v_ext, 2, first, count)
        return value.astype(BF16).astype(F32)

    row_index = lax.broadcasted_iota(jnp.int32, (8, channels), 0)
    p_ext[0:8, :] = jnp.where(row_index < 2, 0.0, product(0, 8))
    for a in range(8, rows, 8):
        p_ext[a : a + 8, :] = product(a, 8)

    rate[...] = rate_in[...]
    decay[...] = jnp.exp(-rate[...])
    coeff[...] = resid_in[...] * jnp.sqrt(one_minus_exp(2.0 * rate[...]))

    step = decay[...]
    low, high = jnp.zeros_like(step), jnp.zeros_like(step)
    for t in range(rows // 2):
        if t % BLOCK == 0:
            prefix[t // BLOCK] = low
            prefix[(t + rows // 2) // BLOCK] = high
        low = step * low + p_ext[t : t + 1, :]
        high = step * high + p_ext[t + rows // 2 : t + rows // 2 + 1, :]
    middle, modes = low, step.shape[0]
    own = high + jnp.exp(rate[...] * (-0.5 * rows)) * middle
    head_gain = jnp.exp(rate[...] * (2.0 - rows))
    whole = jnp.exp(rate[...] * (-1.0 * rows))

    k_first, v_first = k_in[0:16, :].astype(F32), v_in[0:16, :].astype(F32)
    q_last, k_last, v_last = (stream[rows - 16 :, :].astype(F32)[14:16] for stream in (q_in, k_in, v_in))
    z_out[:, :channels] = own.astype(BF16)
    z_out[:, channels:] = packed([k_first[0:2], v_first[0:2], k_last, v_last])
    z_in[z] = z_out[...]
    halo_out[...] = packed([q_last, k_last, v_last, jnp.zeros_like(v_last)])
    pl.semaphore_wait(barrier, len(told))
    z_copies = [put(z_out, z_in.at[z], z_send.at[d - 1], z_recv.at[z], along_z[d - 1]) for d in range(1, RUN)]
    for copy in z_copies:
        copy.start()
    for d in hop_y:
        pl.semaphore_signal(ring_sem, inc=1, device_id=along_y[d - 1], device_id_type=MESH)
    halo = put(halo_out, halo_in, halo_sem.at[0], halo_sem.at[1], after)
    halo.start()
    for w_share in w_shares:
        w_share.start()

    halo.wait_recv()
    inside = jnp.where(ctx > 0, unpacked(halo_in[...]), 0.0)
    k_ext[6:8, :] = inside[2:4, :]
    v_ext[6:8, :] = inside[4:6, :]
    p_ext[0:8, :] = product(0, 8)
    heads[...] = step * p_ext[0:1, :] + p_ext[1:2, :]

    def boundary(last, first):
        value = [1.0, 1.0]
        for n, old, new in ((1, 4, 0), (2, 6, 2)):
            tap = [taps[n, j : j + 1, :] for j in range(3)]
            line = [last[old : old + 1], last[old + 1 : old + 2], first[new : new + 1], first[new + 1 : new + 2]]
            for i in range(2):
                value[i] = value[i] * (tap[0] * line[i + 2] + tap[1] * line[i + 1] + tap[2] * line[i])
        value = [one.astype(BF16).astype(F32) for one in value]
        return step * value[0] + value[1]

    for b in range(1, per):
        span[b] = jnp.exp(rate[...] * (2.0 - BLOCK * b))
        if b > per // 2:
            prefix[b] = prefix[b] + jnp.exp(rate[...] * (1.0 * (per // 2 - b) * BLOCK)) * middle
    prefix[per // 2] = middle
    term = coeff[...]
    for k in range(BLOCK):
        response[k : k + 1, :] = jnp.sum(term, axis=0, keepdims=True)
        term = term * step
    first_gain = coeff[...] * step
    for g, lanes in enumerate(groups):
        for b in range(per):
            decay_b[g, pl.ds(b, modes, stride=per), :] = step[:, lanes]
            gain_b[g, pl.ds(b, modes, stride=per), :] = first_gain[:, lanes]
        q_ext[g, 6:8, :] = inside[0:2, lanes]
        for a in range(0, rows, 16):
            q_ext[g, 8 + a : 24 + a, :] = q_in[a : a + 16, lanes].astype(F32)
            p_group[g, a : a + 16, :] = p_ext[a : a + 16, lanes]
        for r in range(BLOCK):
            total = taps[0, 0:1, lanes] * q_ext[g, pl.ds(8 + r, per, stride=BLOCK), :]
            total = total + taps[0, 1:2, lanes] * q_ext[g, pl.ds(7 + r, per, stride=BLOCK), :]
            total = total + taps[0, 2:3, lanes] * q_ext[g, pl.ds(6 + r, per, stride=BLOCK), :]
            q_feat[r * per : (r + 1) * per, lanes] = total

    def convolve(group, carry):
        lanes = pl.ds(pl.multiple_of(group * LANES, LANES), LANES)
        inputs = [p_group[group, pl.ds(r, per, stride=BLOCK), :] for r in range(BLOCK)]
        for r in range(BLOCK):
            total = response[0:1, lanes] * inputs[r]
            for k in range(1, r + 1):
                total = total + response[k : k + 1, lanes] * inputs[r - k]
            local[r * per : (r + 1) * per, lanes] = total
        return carry

    lax.fori_loop(0, channels // LANES, convolve, 0)

    for d in range(1, RUN):
        there = (z + d) % RUN
        put(z_out, z_in.at[there], z_send.at[d - 1], z_recv.at[there], along_z[d - 1]).wait_recv()
    before_me, total = jnp.zeros_like(step), jnp.zeros_like(step)
    edges = [unpacked(z_in[i, :, channels:]) for i in range(RUN)]
    for i in range(RUN):
        value = z_in[i, :, :channels].astype(F32)
        if i > 0:
            value = value + head_gain * boundary(edges[i - 1], edges[i])
        before_me = jnp.where(i < z, whole * before_me + value, before_me)
        total = whole * total + value

    y_out[:, :channels] = total.astype(BF16)
    row_edges = [edges[0][0:2], edges[0][2:4], edges[RUN - 1][4:6], edges[RUN - 1][6:8]]
    y_out[:, channels:] = packed(row_edges)
    y_in[y] = y_out[...]
    pl.semaphore_wait(ring_sem, len(hop_y))
    y_copies = [put(y_out, y_in.at[y], y_send.at[d - 1], y_recv.at[y], along_y[d - 1]) for d in range(1, rows_y)]
    for d in sorted(range(1, rows_y), key=lambda d: -min(d, rows_y - d)):
        pl.when(y + d < rows_y)(y_copies[d - 1].start)
    row_decay = jnp.exp(rate[...] * (-1.0 * rows * RUN))
    row_gain = jnp.exp(rate[...] * (2.0 - rows * RUN))
    my_gain = jnp.exp(rate[...] * (2.0 - rows * z.astype(F32)))
    for w_load in w_loads:
        w_load.wait()
    for w_share in w_shares:
        w_share.wait()
    for d in range(1, rows_y):
        there = (y + rows_y - d) % rows_y
        arrived = put(y_out, y_in.at[there], y_send.at[d - 1], y_recv.at[there], along_y[d - 1])
        pl.when(y >= d)(arrived.wait_recv)
    state = jnp.zeros_like(step)
    last = jnp.zeros((8, channels), F32)
    row_heads = jnp.zeros_like(step)
    for i in range(rows_y):
        edge = unpacked(y_in[i, :, channels:])
        head = boundary(last, edge)
        row_heads = jnp.where(i == y, head, row_heads)
        value = row_decay * state + row_gain * head + y_in[i, :, :channels].astype(F32)
        state = jnp.where(i < y, value, state)
        last = edge
    state = jnp.where(z > 0, before_me + my_gain * (step * step * state + row_heads), state)
    second = step * step * state + heads[...]
    for b in range(per):
        if b > 0:
            state = prefix[b] + span[b] * second
        for g, lanes in enumerate(groups):
            starts[g, pl.ds(b, modes, stride=per), :] = state[:, lanes]

    steps = BLOCK // chunks
    g_copies, x_copies, h_copies = [], [], []
    for c in range(chunks):

        def gate(group, carry):
            lanes = pl.ds(pl.multiple_of(group * LANES, LANES), LANES)
            shape = (modes, per, LANES)
            ratio = decay_b[group].reshape(shape)
            term = starts[group].reshape(shape)
            if c == 0:
                term = term * gain_b[group].reshape(shape)
            for r in range(c * steps, (c + 1) * steps, 2):
                pair = []
                for one in (r, r + 1):
                    here = slice(one * per, (one + 1) * per)
                    value = local[here, lanes] + jnp.sum(term, axis=0)
                    term = term * ratio
                    pair.append(q_feat[here, lanes] * value.astype(BF16).astype(F32))
                g_own[r * per : (r + 2) * per, lanes] = jnp.concatenate(pair, axis=0).astype(BF16)
            if c + 1 < chunks:
                starts[group] = term.reshape(modes * per, LANES)
            return carry

        lax.fori_loop(0, channels // LANES, gate, 0)
        piece = pl.ds(c * chunk, chunk)
        copy = put(g_own.at[piece], g_par.at[piece], g_send.at[c], g_recv.at[c], other_core)
        copy.start()
        g_copies.append(copy)

    def share(b):
        value = jnp.dot(g_own[...], w_own[b], preferred_element_type=F32)
        return value + jnp.dot(g_par[...], w_par[b], preferred_element_type=F32)

    for c in range(chunks):
        g_copies[c].wait_recv()
    for part, h in enumerate((1 - half, half)):
        copies = []
        for d in (2, 1, 3):
            to = (x + d) % xs
            value = share(to * 2 + h).astype(BF16)
            for c in range(chunks):
                x_out[part, c, d - 1] = value[c * chunk : (c + 1) * chunk]
                copy = put(
                    x_out.at[part, c, d - 1], x_in.at[part, c, d - 1],
                    x_send.at[part, c, d - 1], x_recv.at[part, c, d - 1], along_x[d - 1],
                )
                copies.append((c, copy))
            copies[-chunks][1].start()
        copies.sort(key=lambda item: item[0])
        for c, copy in copies:
            if c > 0:
                copy.start()
            x_copies.append(copy)
    for part, h in enumerate((1 - half, half)):
        x_keep[part] = share(x * 2 + h)

    for part in range(2):
        for c in range(chunks):
            at = (part * chunks + c) * (xs - 1)
            for copy in x_copies[at : at + xs - 1]:
                copy.wait_recv()
            for a in range(0, chunk, 16):
                here = slice(c * chunk + a, c * chunk + a + 16)
                value = x_keep[part, here, :]
                for d in range(1, xs):
                    value = value + x_in[part, c, d - 1, a : a + 16, :].astype(F32)
                if part == 0:
                    h_out[c, a : a + 16, :] = value.astype(BF16)
                else:
                    x_keep[part, here, :] = value
            if part == 0:
                copy = put(h_out.at[c], h_in.at[c], h_send.at[c], h_recv.at[c], other_half)
                copy.start()
                h_copies.append(copy)

    for c in range(chunks):
        h_copies[c].wait_recv()
        for a in range(0, chunk, 16):
            value = x_keep[1, c * chunk + a : c * chunk + a + 16, :] + h_in[c, a : a + 16, :].astype(F32)
            r = (c * chunk + a) // per
            for i in range(16 // per):
                for g in range(cols // LANES):
                    part = value[i * per : (i + 1) * per, g * LANES : (g + 1) * LANES]
                    unperm[g, pl.ds(r + i, per, stride=BLOCK), :] = part
    for copy in [halo] + z_copies + g_copies + x_copies + h_copies:
        copy.wait_send()
    for d in range(1, rows_y):
        pl.when(y + d < rows_y)(y_copies[d - 1].wait_send)
    for g in range(cols // LANES):
        o_ref[:, g * LANES : (g + 1) * LANES] = unperm[g].astype(BF16)


def solution(mesh):
    n_ctx, n_tp = mesh.shape["ctx"], mesh.shape["tp"]
    rows_y, xs = n_ctx // RUN, n_tp // 4
    chunks = 2

    def shards(queries, keys, values, short_taps, long_rates, long_resid, out_weight):
        rows, channels = queries.shape
        modes = long_rates.shape[1]
        out = out_weight.shape[1]
        cols = out // n_tp
        chunk = rows // chunks
        state = (modes, channels)
        message = (modes, channels + channels // 2)
        stream = pltpu.VMEM((rows, channels), BF16)
        sem = pltpu.SemaphoreType.DMA
        return pl.pallas_call(
            kernel,
            name="hyena",
            out_shape=pltpu.VMEM((rows, cols), BF16),
            in_specs=[pl.BlockSpec(memory_space=pltpu.HBM)] * 7,
            out_specs=pl.BlockSpec(memory_space=pltpu.VMEM),
            scratch_shapes=[
                stream, stream, stream,
                pltpu.VMEM(short_taps.shape, F32),
                pltpu.VMEM(state, F32),
                pltpu.VMEM(state, F32),
                pltpu.VMEM((2 * xs, channels, cols), BF16),
                pltpu.VMEM((2 * xs, channels, cols), BF16),
                pltpu.VMEM((channels // LANES, rows + 8, LANES), F32),
                pltpu.VMEM((rows + 8, channels), F32),
                pltpu.VMEM((rows + 8, channels), F32),
                pltpu.VMEM((rows, channels), F32),
                pltpu.VMEM((channels // LANES, rows, LANES), F32),
                pltpu.VMEM((16, channels // 2), BF16),
                pltpu.VMEM((16, channels // 2), BF16),
                pltpu.VMEM(state, F32),
                pltpu.VMEM(state, F32),
                pltpu.VMEM(state, F32),
                pltpu.VMEM(state, F32),
                pltpu.VMEM((rows // BLOCK,) + state, F32),
                pltpu.VMEM((rows // BLOCK,) + state, F32),
                pltpu.VMEM((BLOCK, channels), F32),
                pltpu.VMEM((channels // LANES, modes * (rows // BLOCK), LANES), F32),
                pltpu.VMEM((channels // LANES, modes * (rows // BLOCK), LANES), F32),
                pltpu.VMEM((channels // LANES, modes * (rows // BLOCK), LANES), F32),
                pltpu.VMEM((rows, channels), F32),
                pltpu.VMEM((rows, channels), F32),
                pltpu.VMEM(message, BF16),
                pltpu.VMEM((RUN,) + message, BF16),
                pltpu.VMEM(message, BF16),
                pltpu.VMEM((rows_y,) + message, BF16),
                stream, stream,
                pltpu.VMEM((2, chunks, xs - 1, chunk, cols), BF16),
                pltpu.VMEM((2, chunks, xs - 1, chunk, cols), BF16),
                pltpu.VMEM((2, rows, cols), F32),
                pltpu.VMEM((chunks, chunk, cols), BF16),
                pltpu.VMEM((chunks, chunk, cols), BF16),
                pltpu.VMEM((cols // LANES, rows, LANES), F32),
                sem((6,)),
                sem((2 * xs,)), sem((2 * xs,)), sem((2 * xs,)),
                sem((2,)),
                sem((RUN - 1,)), sem((RUN,)),
                sem((rows_y - 1,)), sem((rows_y,)),
                sem((chunks,)), sem((chunks,)),
                sem((2, chunks, xs - 1)), sem((2, chunks, xs - 1)),
                sem((chunks,)), sem((chunks,)),
                pltpu.SemaphoreType.REGULAR,
            ],
            compiler_params=pltpu.CompilerParams(
                collective_id=0, has_side_effects=True, vmem_limit_bytes=62 * 1024 * 1024
            ),
        )(queries, keys, values, short_taps, long_rates.T, long_resid.T, out_weight)

    return jax.shard_map(
        shards,
        mesh=mesh,
        in_specs=(
            P("ctx", "tp"),
            P("ctx", "tp"),
            P("ctx", "tp"),
            P(None, None, "tp"),
            P("tp", None),
            P("tp", None),
            P("tp", None),
        ),
        out_specs=P("ctx", "tp"),
        check_vma=False,
    )
```

```python
import jax
import jax.numpy as jnp
from jax import lax
from jax.experimental import pallas as pl
from jax.experimental.pallas import tpu as pltpu
from jax.sharding import PartitionSpec as P

MESH = pl.DeviceIdType.MESH
F32 = jnp.float32
BF16 = jnp.bfloat16
RUN = 8
BLOCK = 16
LANES = 128


def one_minus_exp(u):
    series = jnp.ones_like(u)
    for n in range(8, 1, -1):
        series = 1.0 - u * (1.0 / n) * series
    return jnp.where(u < 0.125, u * series, 1.0 - jnp.exp(-u))


def packed(parts):
    value = jnp.concatenate(parts, axis=0)
    width = value.shape[1] // 2
    return jnp.concatenate([value[:, :width], value[:, width:]], axis=0).astype(BF16)


def unpacked(block):
    value = block.astype(F32)
    return jnp.concatenate([value[0:8], value[8:16]], axis=1)


def kernel(
    q_hbm, k_hbm, v_hbm, taps_hbm, rate_hbm, resid_hbm, w_hbm, o_ref,
    q_in, k_in, v_in, taps, rate_in, resid_in, w_own, w_par,
    q_ext, k_ext, v_ext, p_ext, p_group, halo_out, halo_in,
    rate, decay, coeff, heads, prefix, span, response, decay_b, gain_b, starts, local, q_feat,
    z_out, z_in, y_out, y_in, g_own, g_par, x_out, x_in, x_keep, h_out, h_in, unperm,
    in_sem, w_sem, wp_send, wp_recv, halo_sem, z_send, z_recv, y_send, y_recv, g_send, g_recv,
    x_send, x_recv, h_send, h_recv, ring_sem,
):
    rows, channels = q_in.shape
    rows_y, xs = y_in.shape[0], x_in.shape[2] + 1
    chunks, chunk = h_out.shape[0], h_out.shape[1]
    cols = h_out.shape[2]
    per = rows // BLOCK
    ctx, tp = lax.axis_index("ctx"), lax.axis_index("tp")
    y, z = ctx // RUN, ctx % RUN
    x, half, core = tp // 4, (tp // 2) % 2, tp % 2
    n_ctx = rows_y * RUN
    groups = [slice(g * LANES, (g + 1) * LANES) for g in range(channels // LANES)]

    def put(src, dst, send, recv, device):
        return pltpu.make_async_remote_copy(
            src_ref=src, dst_ref=dst, send_sem=send, recv_sem=recv, device_id=device, device_id_type=MESH
        )

    along_z = [(y * RUN + (z + d) % RUN, tp) for d in range(1, RUN)]
    along_y = [(((y + d) % rows_y) * RUN + z, tp) for d in range(1, rows_y)]
    along_x = [(ctx, ((x + d) % xs) * 4 + half * 2 + core) for d in range(1, xs)]
    other_core = (ctx, x * 4 + half * 2 + (1 - core))
    other_half = (ctx, x * 4 + (1 - half) * 2 + core)
    after, before = ((ctx + 1) % n_ctx, tp), ((ctx + n_ctx - 1) % n_ctx, tp)

    far_mate = (y * RUN + (z + RUN // 2) % RUN, other_half[1])
    near_y, hop_y = ([d for d in range(1, rows_y) if min(d, rows_y - d) == reach] for reach in (1, 2))
    near_x = [d for d in range(1, xs) if min(d, xs - d) == 1]
    told = along_z + [other_core, before, far_mate] + [along_y[d - 1] for d in near_y] + [along_x[d - 1] for d in near_x]

    loads = [
        pltpu.make_async_copy(src, dst, in_sem.at[i])
        for i, (src, dst) in enumerate(
            [(k_hbm, k_in), (v_hbm, v_in), (taps_hbm, taps), (rate_hbm, rate_in), (q_hbm, q_in), (resid_hbm, resid_in)]
        )
    ]
    for load in loads:
        load.start()

    barrier = pltpu.get_barrier_semaphore()
    for peer in told:
        pl.semaphore_signal(barrier, inc=1, device_id=peer, device_id_type=MESH)

    blocks = 2 * xs
    w_loads = [
        pltpu.make_async_copy(
            w_hbm.at[:, pl.ds(pl.multiple_of(b * 2 * cols + core * cols, cols), cols)], w_own.at[b], w_sem.at[b]
        )
        for b in range(blocks)
    ]
    w_shares = [
        put(
            w_hbm.at[:, pl.ds(pl.multiple_of(b * 2 * cols + (1 - core) * cols, cols), cols)],
            w_par.at[b], wp_send.at[b], wp_recv.at[b], other_core,
        )
        for b in range(blocks)
    ]

    for load in loads:
        load.wait()
    for w_load in w_loads:
        w_load.start()
    for ext in (k_ext, v_ext):
        ext[0:8, :] = jnp.zeros((8, channels), F32)

    for stream, ext in [(k_in, k_ext), (v_in, v_ext)]:
        for a in range(0, rows, 16):
            ext[8 + a : 24 + a, :] = stream[a : a + 16, :].astype(F32)

    def feature(ext, n, first, count):
        total = taps[n, 0:1, :] * ext[8 + first : 8 + first + count, :]
        total = total + taps[n, 1:2, :] * ext[7 + first : 7 + first + count, :]
        return total + taps[n, 2:3, :] * ext[6 + first : 6 + first + count, :]

    def product(first, count):
        value = feature(k_ext, 1, first, count) * feature(v_ext, 2, first, count)
        return value.astype(BF16).astype(F32)

    row_index = lax.broadcasted_iota(jnp.int32, (8, channels), 0)
    p_ext[0:8, :] = jnp.where(row_index < 2, 0.0, product(0, 8))
    for a in range(8, rows, 8):
        p_ext[a : a + 8, :] = product(a, 8)

    rate[...] = rate_in[...]
    decay[...] = jnp.exp(-rate[...])
    coeff[...] = resid_in[...] * jnp.sqrt(one_minus_exp(2.0 * rate[...]))

    step = decay[...]
    low, high = jnp.zeros_like(step), jnp.zeros_like(step)
    for t in range(rows // 2):
        if t % BLOCK == 0:
            prefix[t // BLOCK] = low
            prefix[(t + rows // 2) // BLOCK] = high
        low = step * low + p_ext[t : t + 1, :]
        high = step * high + p_ext[t + rows // 2 : t + rows // 2 + 1, :]
    middle, modes = low, step.shape[0]
    own = high + jnp.exp(rate[...] * (-0.5 * rows)) * middle
    head_gain = jnp.exp(rate[...] * (2.0 - rows))
    whole = jnp.exp(rate[...] * (-1.0 * rows))

    k_first, v_first = k_in[0:16, :].astype(F32), v_in[0:16, :].astype(F32)
    q_last, k_last, v_last = (stream[rows - 16 :, :].astype(F32)[14:16] for stream in (q_in, k_in, v_in))
    z_out[:, :channels] = own.astype(BF16)
    z_out[:, channels:] = packed([k_first[0:2], v_first[0:2], k_last, v_last])
    z_in[z] = z_out[...]
    halo_out[...] = packed([q_last, k_last, v_last, jnp.zeros_like(v_last)])
    pl.semaphore_wait(barrier, len(told))
    z_copies = [put(z_out, z_in.at[z], z_send.at[d - 1], z_recv.at[z], along_z[d - 1]) for d in range(1, RUN)]
    for copy in z_copies:
        copy.start()
    for d in near_y:
        pl.semaphore_signal(ring_sem.at[0], inc=1, device_id=along_y[d - 1], device_id_type=MESH)
    for d in near_x:
        pl.semaphore_signal(ring_sem.at[1], inc=1, device_id=along_x[d - 1], device_id_type=MESH)
    halo = put(halo_out, halo_in, halo_sem.at[0], halo_sem.at[1], after)
    halo.start()
    for w_share in w_shares:
        w_share.start()

    halo.wait_recv()
    inside = jnp.where(ctx > 0, unpacked(halo_in[...]), 0.0)
    k_ext[6:8, :] = inside[2:4, :]
    v_ext[6:8, :] = inside[4:6, :]
    p_ext[0:8, :] = product(0, 8)
    heads[...] = step * p_ext[0:1, :] + p_ext[1:2, :]

    def boundary(last, first):
        value = [1.0, 1.0]
        for n, old, new in ((1, 4, 0), (2, 6, 2)):
            tap = [taps[n, j : j + 1, :] for j in range(3)]
            line = [last[old : old + 1], last[old + 1 : old + 2], first[new : new + 1], first[new + 1 : new + 2]]
            for i in range(2):
                value[i] = value[i] * (tap[0] * line[i + 2] + tap[1] * line[i + 1] + tap[2] * line[i])
        value = [one.astype(BF16).astype(F32) for one in value]
        return step * value[0] + value[1]

    for b in range(1, per):
        span[b] = jnp.exp(rate[...] * (2.0 - BLOCK * b))
        if b > per // 2:
            prefix[b] = prefix[b] + jnp.exp(rate[...] * (1.0 * (per // 2 - b) * BLOCK)) * middle
    prefix[per // 2] = middle
    term = coeff[...]
    for k in range(BLOCK):
        response[k : k + 1, :] = jnp.sum(term, axis=0, keepdims=True)
        term = term * step
    first_gain = coeff[...] * step
    for g, lanes in enumerate(groups):
        for b in range(per):
            decay_b[g, pl.ds(b, modes, stride=per), :] = step[:, lanes]
            gain_b[g, pl.ds(b, modes, stride=per), :] = first_gain[:, lanes]
        q_ext[g, 6:8, :] = inside[0:2, lanes]
        for a in range(0, rows, 16):
            q_ext[g, 8 + a : 24 + a, :] = q_in[a : a + 16, lanes].astype(F32)
            p_group[g, a : a + 16, :] = p_ext[a : a + 16, lanes]
        for r in range(BLOCK):
            total = taps[0, 0:1, lanes] * q_ext[g, pl.ds(8 + r, per, stride=BLOCK), :]
            total = total + taps[0, 1:2, lanes] * q_ext[g, pl.ds(7 + r, per, stride=BLOCK), :]
            total = total + taps[0, 2:3, lanes] * q_ext[g, pl.ds(6 + r, per, stride=BLOCK), :]
            q_feat[r * per : (r + 1) * per, lanes] = total

    def convolve(group, carry):
        lanes = pl.ds(pl.multiple_of(group * LANES, LANES), LANES)
        inputs = [p_group[group, pl.ds(r, per, stride=BLOCK), :] for r in range(BLOCK)]
        for r in range(BLOCK):
            total = response[0:1, lanes] * inputs[r]
            for k in range(1, r + 1):
                total = total + response[k : k + 1, lanes] * inputs[r - k]
            local[r * per : (r + 1) * per, lanes] = total
        return carry

    lax.fori_loop(0, channels // LANES, convolve, 0)

    pl.semaphore_wait(ring_sem.at[0], len(near_y))
    for d in hop_y:
        pl.semaphore_signal(ring_sem.at[2], inc=1, device_id=along_y[d - 1], device_id_type=MESH)
    pl.semaphore_wait(ring_sem.at[1], len(near_x))
    for d in range(1, RUN):
        there = (z + d) % RUN
        put(z_out, z_in.at[there], z_send.at[d - 1], z_recv.at[there], along_z[d - 1]).wait_recv()
    before_me, total = jnp.zeros_like(step), jnp.zeros_like(step)
    edges = [unpacked(z_in[i, :, channels:]) for i in range(RUN)]
    for i in range(RUN):
        value = z_in[i, :, :channels].astype(F32)
        if i > 0:
            value = value + head_gain * boundary(edges[i - 1], edges[i])
        before_me = jnp.where(i < z, whole * before_me + value, before_me)
        total = whole * total + value

    y_out[:, :channels] = total.astype(BF16)
    row_edges = [edges[0][0:2], edges[0][2:4], edges[RUN - 1][4:6], edges[RUN - 1][6:8]]
    y_out[:, channels:] = packed(row_edges)
    y_in[y] = y_out[...]
    pl.semaphore_wait(ring_sem.at[2], len(hop_y))
    y_copies = [put(y_out, y_in.at[y], y_send.at[d - 1], y_recv.at[y], along_y[d - 1]) for d in range(1, rows_y)]
    for d in range(1, rows_y):
        pl.when(y + d < rows_y)(y_copies[d - 1].start)
    row_decay = jnp.exp(rate[...] * (-1.0 * rows * RUN))
    row_gain = jnp.exp(rate[...] * (2.0 - rows * RUN))
    my_gain = jnp.exp(rate[...] * (2.0 - rows * z.astype(F32)))
    for w_load in w_loads:
        w_load.wait()
    for w_share in w_shares:
        w_share.wait()
    for d in range(1, rows_y):
        there = (y + rows_y - d) % rows_y
        arrived = put(y_out, y_in.at[there], y_send.at[d - 1], y_recv.at[there], along_y[d - 1])
        pl.when(y >= d)(arrived.wait_recv)
    state = jnp.zeros_like(step)
    last = jnp.zeros((8, channels), F32)
    row_heads = jnp.zeros_like(step)
    for i in range(rows_y):
        edge = unpacked(y_in[i, :, channels:])
        head = boundary(last, edge)
        row_heads = jnp.where(i == y, head, row_heads)
        value = row_decay * state + row_gain * head + y_in[i, :, :channels].astype(F32)
        state = jnp.where(i < y, value, state)
        last = edge
    state = jnp.where(z > 0, before_me + my_gain * (step * step * state + row_heads), state)
    second = step * step * state + heads[...]
    for b in range(per):
        if b > 0:
            state = prefix[b] + span[b] * second
        for g, lanes in enumerate(groups):
            starts[g, pl.ds(b, modes, stride=per), :] = state[:, lanes]

    steps = BLOCK // chunks
    g_copies, x_copies, h_copies = [], [], []
    for c in range(chunks):

        def gate(group, carry):
            lanes = pl.ds(pl.multiple_of(group * LANES, LANES), LANES)
            shape = (modes, per, LANES)
            ratio = decay_b[group].reshape(shape)
            term = starts[group].reshape(shape)
            if c == 0:
                term = term * gain_b[group].reshape(shape)
            for r in range(c * steps, (c + 1) * steps, 2):
                pair = []
                for one in (r, r + 1):
                    here = slice(one * per, (one + 1) * per)
                    value = local[here, lanes] + jnp.sum(term, axis=0)
                    term = term * ratio
                    pair.append(q_feat[here, lanes] * value.astype(BF16).astype(F32))
                g_own[r * per : (r + 2) * per, lanes] = jnp.concatenate(pair, axis=0).astype(BF16)
            if c + 1 < chunks:
                starts[group] = term.reshape(modes * per, LANES)
            return carry

        lax.fori_loop(0, channels // LANES, gate, 0)
        piece = pl.ds(c * chunk, chunk)
        copy = put(g_own.at[piece], g_par.at[piece], g_send.at[c], g_recv.at[c], other_core)
        copy.start()
        g_copies.append(copy)

    def share(b):
        value = jnp.dot(g_own[...], w_own[b], preferred_element_type=F32)
        return value + jnp.dot(g_par[...], w_par[b], preferred_element_type=F32)

    for c in range(chunks):
        g_copies[c].wait_recv()
    waiting = []
    for part, h in enumerate((1 - half, half)):
        copies = []
        for d in (2, 1, 3):
            to = (x + d) % xs
            value = share(to * 2 + h).astype(BF16)
            for c in range(chunks):
                x_out[part, c, d - 1] = value[c * chunk : (c + 1) * chunk]
                copy = put(
                    x_out.at[part, c, d - 1], x_in.at[part, c, d - 1],
                    x_send.at[part, c, d - 1], x_recv.at[part, c, d - 1], along_x[d - 1],
                )
                copies.append((c, copy))
            if part == 0:
                copies[-chunks][1].start()
        copies.sort(key=lambda item: item[0])
        for c, copy in copies:
            if part == 0 and c > 0:
                copy.start()
            if part == 1:
                waiting.append(copy)
            x_copies.append(copy)
        if part == 0:
            x_keep[0] = share(x * 2 + h)
    x_keep[1] = share(x * 2 + half)

    for part in range(2):
        for c in range(chunks):
            at = (part * chunks + c) * (xs - 1)
            for copy in x_copies[at : at + xs - 1]:
                copy.wait_recv()
            for a in range(0, chunk, 16):
                here = slice(c * chunk + a, c * chunk + a + 16)
                value = x_keep[part, here, :]
                for d in range(1, xs):
                    value = value + x_in[part, c, d - 1, a : a + 16, :].astype(F32)
                if part == 0:
                    h_out[c, a : a + 16, :] = value.astype(BF16)
                else:
                    x_keep[part, here, :] = value
            if part == 0:
                copy = put(h_out.at[c], h_in.at[c], h_send.at[c], h_recv.at[c], other_half)
                copy.start()
                h_copies.append(copy)
                if c == chunks - 1:
                    for copy in waiting:
                        copy.start()

    for c in range(chunks):
        h_copies[c].wait_recv()
        for a in range(0, chunk, 16):
            value = x_keep[1, c * chunk + a : c * chunk + a + 16, :] + h_in[c, a : a + 16, :].astype(F32)
            r = (c * chunk + a) // per
            for i in range(16 // per):
                for g in range(cols // LANES):
                    part = value[i * per : (i + 1) * per, g * LANES : (g + 1) * LANES]
                    unperm[g, pl.ds(r + i, per, stride=BLOCK), :] = part
    for copy in [halo] + z_copies + g_copies + x_copies + h_copies:
        copy.wait_send()
    for d in range(1, rows_y):
        pl.when(y + d < rows_y)(y_copies[d - 1].wait_send)
    for g in range(cols // LANES):
        o_ref[:, g * LANES : (g + 1) * LANES] = unperm[g].astype(BF16)


def solution(mesh):
    n_ctx, n_tp = mesh.shape["ctx"], mesh.shape["tp"]
    rows_y, xs = n_ctx // RUN, n_tp // 4
    chunks = 2

    def shards(queries, keys, values, short_taps, long_rates, long_resid, out_weight):
        rows, channels = queries.shape
        modes = long_rates.shape[1]
        out = out_weight.shape[1]
        cols = out // n_tp
        chunk = rows // chunks
        state = (modes, channels)
        message = (modes, channels + channels // 2)
        stream = pltpu.VMEM((rows, channels), BF16)
        sem = pltpu.SemaphoreType.DMA
        return pl.pallas_call(
            kernel,
            name="hyena",
            out_shape=pltpu.VMEM((rows, cols), BF16),
            in_specs=[pl.BlockSpec(memory_space=pltpu.HBM)] * 7,
            out_specs=pl.BlockSpec(memory_space=pltpu.VMEM),
            scratch_shapes=[
                stream, stream, stream,
                pltpu.VMEM(short_taps.shape, F32),
                pltpu.VMEM(state, F32),
                pltpu.VMEM(state, F32),
                pltpu.VMEM((2 * xs, channels, cols), BF16),
                pltpu.VMEM((2 * xs, channels, cols), BF16),
                pltpu.VMEM((channels // LANES, rows + 8, LANES), F32),
                pltpu.VMEM((rows + 8, channels), F32),
                pltpu.VMEM((rows + 8, channels), F32),
                pltpu.VMEM((rows, channels), F32),
                pltpu.VMEM((channels // LANES, rows, LANES), F32),
                pltpu.VMEM((16, channels // 2), BF16),
                pltpu.VMEM((16, channels // 2), BF16),
                pltpu.VMEM(state, F32),
                pltpu.VMEM(state, F32),
                pltpu.VMEM(state, F32),
                pltpu.VMEM(state, F32),
                pltpu.VMEM((rows // BLOCK,) + state, F32),
                pltpu.VMEM((rows // BLOCK,) + state, F32),
                pltpu.VMEM((BLOCK, channels), F32),
                pltpu.VMEM((channels // LANES, modes * (rows // BLOCK), LANES), F32),
                pltpu.VMEM((channels // LANES, modes * (rows // BLOCK), LANES), F32),
                pltpu.VMEM((channels // LANES, modes * (rows // BLOCK), LANES), F32),
                pltpu.VMEM((rows, channels), F32),
                pltpu.VMEM((rows, channels), F32),
                pltpu.VMEM(message, BF16),
                pltpu.VMEM((RUN,) + message, BF16),
                pltpu.VMEM(message, BF16),
                pltpu.VMEM((rows_y,) + message, BF16),
                stream, stream,
                pltpu.VMEM((2, chunks, xs - 1, chunk, cols), BF16),
                pltpu.VMEM((2, chunks, xs - 1, chunk, cols), BF16),
                pltpu.VMEM((2, rows, cols), F32),
                pltpu.VMEM((chunks, chunk, cols), BF16),
                pltpu.VMEM((chunks, chunk, cols), BF16),
                pltpu.VMEM((cols // LANES, rows, LANES), F32),
                sem((6,)),
                sem((2 * xs,)), sem((2 * xs,)), sem((2 * xs,)),
                sem((2,)),
                sem((RUN - 1,)), sem((RUN,)),
                sem((rows_y - 1,)), sem((rows_y,)),
                sem((chunks,)), sem((chunks,)),
                sem((2, chunks, xs - 1)), sem((2, chunks, xs - 1)),
                sem((chunks,)), sem((chunks,)),
                pltpu.SemaphoreType.REGULAR((3,)),
            ],
            compiler_params=pltpu.CompilerParams(
                collective_id=0, has_side_effects=True, vmem_limit_bytes=62 * 1024 * 1024
            ),
        )(queries, keys, values, short_taps, long_rates.T, long_resid.T, out_weight)

    return jax.shard_map(
        shards,
        mesh=mesh,
        in_specs=(
            P("ctx", "tp"),
            P("ctx", "tp"),
            P("ctx", "tp"),
            P(None, None, "tp"),
            P("tp", None),
            P("tp", None),
            P("tp", None),
        ),
        out_specs=P("ctx", "tp"),
        check_vma=False,
    )
```

```python
import jax
import jax.numpy as jnp
from jax import lax
from jax.experimental import pallas as pl
from jax.experimental.pallas import tpu as pltpu
from jax.sharding import PartitionSpec as P

MESH = pl.DeviceIdType.MESH
F32 = jnp.float32
BF16 = jnp.bfloat16
RUN = 8
BLOCK = 16
LANES = 128


def one_minus_exp(u):
    series = jnp.ones_like(u)
    for n in range(8, 1, -1):
        series = 1.0 - u * (1.0 / n) * series
    return jnp.where(u < 0.125, u * series, 1.0 - jnp.exp(-u))


def packed(parts):
    value = jnp.concatenate(parts, axis=0)
    width = value.shape[1] // 2
    return jnp.concatenate([value[:, :width], value[:, width:]], axis=0).astype(BF16)


def unpacked(block):
    value = block.astype(F32)
    return jnp.concatenate([value[0:8], value[8:16]], axis=1)


def kernel(
    q_hbm, k_hbm, v_hbm, taps_hbm, rate_hbm, resid_hbm, w_hbm, o_ref,
    q_in, k_in, v_in, taps, rate_in, resid_in, w_own, w_par,
    q_ext, k_ext, v_ext, p_ext, p_group, halo_out, halo_in,
    rate, decay, coeff, heads, prefix, span, response, decay_b, gain_b, starts, local, q_feat,
    z_out, z_in, y_out, y_in, g_own, g_par, x_out, x_in, x_keep, h_out, h_in, unperm,
    in_sem, w_sem, wp_send, wp_recv, halo_sem, z_send, z_recv, y_send, y_recv, g_send, g_recv,
    x_send, x_recv, h_send, h_recv, ring_sem,
):
    rows, channels = q_in.shape
    rows_y, xs = y_in.shape[0], x_in.shape[2] + 1
    chunks, chunk = h_out.shape[0], h_out.shape[1]
    cols = h_out.shape[2]
    per = rows // BLOCK
    ctx, tp = lax.axis_index("ctx"), lax.axis_index("tp")
    y, z = ctx // RUN, ctx % RUN
    x, half, core = tp // 4, (tp // 2) % 2, tp % 2
    n_ctx = rows_y * RUN
    groups = [slice(g * LANES, (g + 1) * LANES) for g in range(channels // LANES)]

    def put(src, dst, send, recv, device):
        return pltpu.make_async_remote_copy(
            src_ref=src, dst_ref=dst, send_sem=send, recv_sem=recv, device_id=device, device_id_type=MESH
        )

    along_z = [(y * RUN + (z + d) % RUN, tp) for d in range(1, RUN)]
    along_y = [(((y + d) % rows_y) * RUN + z, tp) for d in range(1, rows_y)]
    along_x = [(ctx, ((x + d) % xs) * 4 + half * 2 + core) for d in range(1, xs)]
    other_core = (ctx, x * 4 + half * 2 + (1 - core))
    other_half = (ctx, x * 4 + (1 - half) * 2 + core)
    after, before = ((ctx + 1) % n_ctx, tp), ((ctx + n_ctx - 1) % n_ctx, tp)

    far_mate = (y * RUN + (z + RUN // 2) % RUN, other_half[1])
    near_y = [d for d in range(1, rows_y) if min(d, rows_y - d) <= 2]
    hop_y = [d for d in range(1, rows_y) if min(d, rows_y - d) == 2]
    told = along_z + along_x + [other_core, before, far_mate] + [along_y[d - 1] for d in near_y]

    loads = [
        pltpu.make_async_copy(src, dst, in_sem.at[i])
        for i, (src, dst) in enumerate(
            [(k_hbm, k_in), (v_hbm, v_in), (taps_hbm, taps), (rate_hbm, rate_in), (q_hbm, q_in), (resid_hbm, resid_in)]
        )
    ]
    for load in loads:
        load.start()

    barrier = pltpu.get_barrier_semaphore()
    for peer in told:
        pl.semaphore_signal(barrier, inc=1, device_id=peer, device_id_type=MESH)

    blocks = 2 * xs
    w_loads = [
        pltpu.make_async_copy(
            w_hbm.at[:, pl.ds(pl.multiple_of(b * 2 * cols + core * cols, cols), cols)], w_own.at[b], w_sem.at[b]
        )
        for b in range(blocks)
    ]
    w_shares = [
        put(
            w_hbm.at[:, pl.ds(pl.multiple_of(b * 2 * cols + (1 - core) * cols, cols), cols)],
            w_par.at[b], wp_send.at[b], wp_recv.at[b], other_core,
        )
        for b in range(blocks)
    ]

    for load in loads:
        load.wait()
    for w_load in w_loads:
        w_load.start()
    for ext in (k_ext, v_ext):
        ext[0:8, :] = jnp.zeros((8, channels), F32)

    for stream, ext in [(k_in, k_ext), (v_in, v_ext)]:
        for a in range(0, rows, 16):
            ext[8 + a : 24 + a, :] = stream[a : a + 16, :].astype(F32)

    def feature(ext, n, first, count):
        total = taps[n, 0:1, :] * ext[8 + first : 8 + first + count, :]
        total = total + taps[n, 1:2, :] * ext[7 + first : 7 + first + count, :]
        return total + taps[n, 2:3, :] * ext[6 + first : 6 + first + count, :]

    def product(first, count):
        value = feature(k_ext, 1, first, count) * feature(v_ext, 2, first, count)
        return value.astype(BF16).astype(F32)

    row_index = lax.broadcasted_iota(jnp.int32, (8, channels), 0)
    p_ext[0:8, :] = jnp.where(row_index < 2, 0.0, product(0, 8))
    for a in range(8, rows, 8):
        p_ext[a : a + 8, :] = product(a, 8)

    rate[...] = rate_in[...]
    decay[...] = jnp.exp(-rate[...])
    coeff[...] = resid_in[...] * jnp.sqrt(one_minus_exp(2.0 * rate[...]))

    step = decay[...]
    low, high = jnp.zeros_like(step), jnp.zeros_like(step)
    for t in range(rows // 2):
        if t % BLOCK == 0:
            prefix[t // BLOCK] = low
            prefix[(t + rows // 2) // BLOCK] = high
        low = step * low + p_ext[t : t + 1, :]
        high = step * high + p_ext[t + rows // 2 : t + rows // 2 + 1, :]
    middle, modes = low, step.shape[0]
    own = high + jnp.exp(rate[...] * (-0.5 * rows)) * middle
    head_gain = jnp.exp(rate[...] * (2.0 - rows))
    whole = jnp.exp(rate[...] * (-1.0 * rows))

    k_first, v_first = k_in[0:16, :].astype(F32), v_in[0:16, :].astype(F32)
    q_last, k_last, v_last = (stream[rows - 16 :, :].astype(F32)[14:16] for stream in (q_in, k_in, v_in))
    z_out[:, :channels] = own.astype(BF16)
    z_out[:, channels:] = packed([k_first[0:2], v_first[0:2], k_last, v_last])
    z_in[z] = z_out[...]
    halo_out[...] = packed([q_last, k_last, v_last, jnp.zeros_like(v_last)])
    pl.semaphore_wait(barrier, len(told))
    z_copies = [put(z_out, z_in.at[z], z_send.at[d - 1], z_recv.at[z], along_z[d - 1]) for d in range(1, RUN)]
    for copy in z_copies:
        copy.start()
    for d in hop_y:
        pl.semaphore_signal(ring_sem, inc=1, device_id=along_y[d - 1], device_id_type=MESH)
    halo = put(halo_out, halo_in, halo_sem.at[0], halo_sem.at[1], after)
    halo.start()
    for w_share in w_shares:
        w_share.start()

    def boundary(last, first):
        value = [1.0, 1.0]
        for n, old, new in ((1, 4, 0), (2, 6, 2)):
            tap = [taps[n, j : j + 1, :] for j in range(3)]
            line = [last[old : old + 1], last[old + 1 : old + 2], first[new : new + 1], first[new + 1 : new + 2]]
            for i in range(2):
                value[i] = value[i] * (tap[0] * line[i + 2] + tap[1] * line[i + 1] + tap[2] * line[i])
        value = [one.astype(BF16).astype(F32) for one in value]
        return step * value[0] + value[1]

    for b in range(1, per):
        span[b] = jnp.exp(rate[...] * (2.0 - BLOCK * b))
        if b > per // 2:
            prefix[b] = prefix[b] + jnp.exp(rate[...] * (1.0 * (per // 2 - b) * BLOCK)) * middle
    prefix[per // 2] = middle
    term = coeff[...]
    for k in range(BLOCK):
        response[k : k + 1, :] = jnp.sum(term, axis=0, keepdims=True)
        term = term * step
    first_gain = coeff[...] * step
    for g, lanes in enumerate(groups):
        for b in range(per):
            decay_b[g, pl.ds(b, modes, stride=per), :] = step[:, lanes]
            gain_b[g, pl.ds(b, modes, stride=per), :] = first_gain[:, lanes]

    for d in range(1, RUN):
        there = (z + d) % RUN
        put(z_out, z_in.at[there], z_send.at[d - 1], z_recv.at[there], along_z[d - 1]).wait_recv()
    before_me, total = jnp.zeros_like(step), jnp.zeros_like(step)
    edges = [unpacked(z_in[i, :, channels:]) for i in range(RUN)]
    for i in range(RUN):
        value = z_in[i, :, :channels].astype(F32)
        if i > 0:
            value = value + head_gain * boundary(edges[i - 1], edges[i])
        before_me = jnp.where(i < z, whole * before_me + value, before_me)
        total = whole * total + value

    y_out[:, :channels] = total.astype(BF16)
    row_edges = [edges[0][0:2], edges[0][2:4], edges[RUN - 1][4:6], edges[RUN - 1][6:8]]
    y_out[:, channels:] = packed(row_edges)
    y_in[y] = y_out[...]
    pl.semaphore_wait(ring_sem, len(hop_y))
    y_copies = [put(y_out, y_in.at[y], y_send.at[d - 1], y_recv.at[y], along_y[d - 1]) for d in range(1, rows_y)]
    for d in sorted(range(1, rows_y), key=lambda d: (d != 1, -min(d, rows_y - d))):
        pl.when(y + d < rows_y)(y_copies[d - 1].start)
    halo.wait_recv()
    inside = jnp.where(ctx > 0, unpacked(halo_in[...]), 0.0)
    k_ext[6:8, :] = inside[2:4, :]
    v_ext[6:8, :] = inside[4:6, :]
    p_ext[0:8, :] = product(0, 8)
    heads[...] = step * p_ext[0:1, :] + p_ext[1:2, :]
    for g, lanes in enumerate(groups):
        q_ext[g, 6:8, :] = inside[0:2, lanes]
        for a in range(0, rows, 16):
            q_ext[g, 8 + a : 24 + a, :] = q_in[a : a + 16, lanes].astype(F32)
            p_group[g, a : a + 16, :] = p_ext[a : a + 16, lanes]
        for r in range(BLOCK):
            total = taps[0, 0:1, lanes] * q_ext[g, pl.ds(8 + r, per, stride=BLOCK), :]
            total = total + taps[0, 1:2, lanes] * q_ext[g, pl.ds(7 + r, per, stride=BLOCK), :]
            total = total + taps[0, 2:3, lanes] * q_ext[g, pl.ds(6 + r, per, stride=BLOCK), :]
            q_feat[r * per : (r + 1) * per, lanes] = total

    def convolve(group, carry):
        lanes = pl.ds(pl.multiple_of(group * LANES, LANES), LANES)
        inputs = [p_group[group, pl.ds(r, per, stride=BLOCK), :] for r in range(BLOCK)]
        for r in range(BLOCK):
            total = response[0:1, lanes] * inputs[r]
            for k in range(1, r + 1):
                total = total + response[k : k + 1, lanes] * inputs[r - k]
            local[r * per : (r + 1) * per, lanes] = total
        return carry

    lax.fori_loop(0, channels // LANES, convolve, 0)

    row_decay = jnp.exp(rate[...] * (-1.0 * rows * RUN))
    row_gain = jnp.exp(rate[...] * (2.0 - rows * RUN))
    my_gain = jnp.exp(rate[...] * (2.0 - rows * z.astype(F32)))
    for d in range(1, rows_y):
        there = (y + rows_y - d) % rows_y
        arrived = put(y_out, y_in.at[there], y_send.at[d - 1], y_recv.at[there], along_y[d - 1])
        pl.when(y >= d)(arrived.wait_recv)
    state = jnp.zeros_like(step)
    last = jnp.zeros((8, channels), F32)
    row_heads = jnp.zeros_like(step)
    for i in range(rows_y):
        edge = unpacked(y_in[i, :, channels:])
        head = boundary(last, edge)
        row_heads = jnp.where(i == y, head, row_heads)
        value = row_decay * state + row_gain * head + y_in[i, :, :channels].astype(F32)
        state = jnp.where(i < y, value, state)
        last = edge
    state = jnp.where(z > 0, before_me + my_gain * (step * step * state + row_heads), state)
    second = step * step * state + heads[...]
    for b in range(per):
        if b > 0:
            state = prefix[b] + span[b] * second
        for g, lanes in enumerate(groups):
            starts[g, pl.ds(b, modes, stride=per), :] = state[:, lanes]

    steps = BLOCK // chunks
    g_copies, x_copies, h_copies = [], [], []
    for c in range(chunks):

        def gate(group, carry):
            lanes = pl.ds(pl.multiple_of(group * LANES, LANES), LANES)
            shape = (modes, per, LANES)
            ratio = decay_b[group].reshape(shape)
            term = starts[group].reshape(shape)
            if c == 0:
                term = term * gain_b[group].reshape(shape)
            for r in range(c * steps, (c + 1) * steps, 2):
                pair = []
                for one in (r, r + 1):
                    here = slice(one * per, (one + 1) * per)
                    value = local[here, lanes] + jnp.sum(term, axis=0)
                    term = term * ratio
                    pair.append(q_feat[here, lanes] * value.astype(BF16).astype(F32))
                g_own[r * per : (r + 2) * per, lanes] = jnp.concatenate(pair, axis=0).astype(BF16)
            if c + 1 < chunks:
                starts[group] = term.reshape(modes * per, LANES)
            return carry

        lax.fori_loop(0, channels // LANES, gate, 0)
        piece = pl.ds(c * chunk, chunk)
        copy = put(g_own.at[piece], g_par.at[piece], g_send.at[c], g_recv.at[c], other_core)
        copy.start()
        g_copies.append(copy)

    def share(b):
        value = jnp.dot(g_own[...], w_own[b], preferred_element_type=F32)
        return value + jnp.dot(g_par[...], w_par[b], preferred_element_type=F32)

    for w_load in w_loads:
        w_load.wait()
    for w_share in w_shares:
        w_share.wait()
    for c in range(chunks):
        g_copies[c].wait_recv()
    waiting = []
    for part, h in enumerate((1 - half, half)):
        copies = []
        for d in (2, 1, 3):
            to = (x + d) % xs
            value = share(to * 2 + h).astype(BF16)
            for c in range(chunks):
                x_out[part, c, d - 1] = value[c * chunk : (c + 1) * chunk]
                copy = put(
                    x_out.at[part, c, d - 1], x_in.at[part, c, d - 1],
                    x_send.at[part, c, d - 1], x_recv.at[part, c, d - 1], along_x[d - 1],
                )
                copies.append((c, copy))
            if part == 0:
                copies[-chunks][1].start()
        copies.sort(key=lambda item: item[0])
        for c, copy in copies:
            if part == 0 and c > 0:
                copy.start()
            if part == 1:
                waiting.append(copy)
            x_copies.append(copy)
        if part == 0:
            x_keep[0] = share(x * 2 + h)
    x_keep[1] = share(x * 2 + half)

    for part in range(2):
        for c in range(chunks):
            at = (part * chunks + c) * (xs - 1)
            for copy in x_copies[at : at + xs - 1]:
                copy.wait_recv()
            for a in range(0, chunk, 16):
                here = slice(c * chunk + a, c * chunk + a + 16)
                value = x_keep[part, here, :]
                for d in range(1, xs):
                    value = value + x_in[part, c, d - 1, a : a + 16, :].astype(F32)
                if part == 0:
                    h_out[c, a : a + 16, :] = value.astype(BF16)
                else:
                    x_keep[part, here, :] = value
            if part == 0:
                copy = put(h_out.at[c], h_in.at[c], h_send.at[c], h_recv.at[c], other_half)
                copy.start()
                h_copies.append(copy)
                if c == chunks - 1:
                    for copy in waiting:
                        copy.start()

    for c in range(chunks):
        h_copies[c].wait_recv()
        for a in range(0, chunk, 16):
            value = x_keep[1, c * chunk + a : c * chunk + a + 16, :] + h_in[c, a : a + 16, :].astype(F32)
            r = (c * chunk + a) // per
            for i in range(16 // per):
                for g in range(cols // LANES):
                    part = value[i * per : (i + 1) * per, g * LANES : (g + 1) * LANES]
                    unperm[g, pl.ds(r + i, per, stride=BLOCK), :] = part
    for copy in [halo] + z_copies + g_copies + x_copies + h_copies:
        copy.wait_send()
    for d in range(1, rows_y):
        pl.when(y + d < rows_y)(y_copies[d - 1].wait_send)
    for g in range(cols // LANES):
        o_ref[:, g * LANES : (g + 1) * LANES] = unperm[g].astype(BF16)


def solution(mesh):
    n_ctx, n_tp = mesh.shape["ctx"], mesh.shape["tp"]
    rows_y, xs = n_ctx // RUN, n_tp // 4
    chunks = 2

    def shards(queries, keys, values, short_taps, long_rates, long_resid, out_weight):
        rows, channels = queries.shape
        modes = long_rates.shape[1]
        out = out_weight.shape[1]
        cols = out // n_tp
        chunk = rows // chunks
        state = (modes, channels)
        message = (modes, channels + channels // 2)
        stream = pltpu.VMEM((rows, channels), BF16)
        sem = pltpu.SemaphoreType.DMA
        return pl.pallas_call(
            kernel,
            name="hyena",
            out_shape=pltpu.VMEM((rows, cols), BF16),
            in_specs=[pl.BlockSpec(memory_space=pltpu.HBM)] * 7,
            out_specs=pl.BlockSpec(memory_space=pltpu.VMEM),
            scratch_shapes=[
                stream, stream, stream,
                pltpu.VMEM(short_taps.shape, F32),
                pltpu.VMEM(state, F32),
                pltpu.VMEM(state, F32),
                pltpu.VMEM((2 * xs, channels, cols), BF16),
                pltpu.VMEM((2 * xs, channels, cols), BF16),
                pltpu.VMEM((channels // LANES, rows + 8, LANES), F32),
                pltpu.VMEM((rows + 8, channels), F32),
                pltpu.VMEM((rows + 8, channels), F32),
                pltpu.VMEM((rows, channels), F32),
                pltpu.VMEM((channels // LANES, rows, LANES), F32),
                pltpu.VMEM((16, channels // 2), BF16),
                pltpu.VMEM((16, channels // 2), BF16),
                pltpu.VMEM(state, F32),
                pltpu.VMEM(state, F32),
                pltpu.VMEM(state, F32),
                pltpu.VMEM(state, F32),
                pltpu.VMEM((rows // BLOCK,) + state, F32),
                pltpu.VMEM((rows // BLOCK,) + state, F32),
                pltpu.VMEM((BLOCK, channels), F32),
                pltpu.VMEM((channels // LANES, modes * (rows // BLOCK), LANES), F32),
                pltpu.VMEM((channels // LANES, modes * (rows // BLOCK), LANES), F32),
                pltpu.VMEM((channels // LANES, modes * (rows // BLOCK), LANES), F32),
                pltpu.VMEM((rows, channels), F32),
                pltpu.VMEM((rows, channels), F32),
                pltpu.VMEM(message, BF16),
                pltpu.VMEM((RUN,) + message, BF16),
                pltpu.VMEM(message, BF16),
                pltpu.VMEM((rows_y,) + message, BF16),
                stream, stream,
                pltpu.VMEM((2, chunks, xs - 1, chunk, cols), BF16),
                pltpu.VMEM((2, chunks, xs - 1, chunk, cols), BF16),
                pltpu.VMEM((2, rows, cols), F32),
                pltpu.VMEM((chunks, chunk, cols), BF16),
                pltpu.VMEM((chunks, chunk, cols), BF16),
                pltpu.VMEM((cols // LANES, rows, LANES), F32),
                sem((6,)),
                sem((2 * xs,)), sem((2 * xs,)), sem((2 * xs,)),
                sem((2,)),
                sem((RUN - 1,)), sem((RUN,)),
                sem((rows_y - 1,)), sem((rows_y,)),
                sem((chunks,)), sem((chunks,)),
                sem((2, chunks, xs - 1)), sem((2, chunks, xs - 1)),
                sem((chunks,)), sem((chunks,)),
                pltpu.SemaphoreType.REGULAR,
            ],
            compiler_params=pltpu.CompilerParams(
                collective_id=0, has_side_effects=True, vmem_limit_bytes=62 * 1024 * 1024
            ),
        )(queries, keys, values, short_taps, long_rates.T, long_resid.T, out_weight)

    return jax.shard_map(
        shards,
        mesh=mesh,
        in_specs=(
            P("ctx", "tp"),
            P("ctx", "tp"),
            P("ctx", "tp"),
            P(None, None, "tp"),
            P("tp", None),
            P("tp", None),
            P("tp", None),
        ),
        out_specs=P("ctx", "tp"),
        check_vma=False,
    )
```

```python
import jax
import jax.numpy as jnp
from jax import lax
from jax.experimental import pallas as pl
from jax.experimental.pallas import tpu as pltpu
from jax.sharding import PartitionSpec as P

MESH = pl.DeviceIdType.MESH
F32 = jnp.float32
BF16 = jnp.bfloat16
RUN = 8
BLOCK = 16
LANES = 128


def one_minus_exp(u):
    series = jnp.ones_like(u)
    for n in range(8, 1, -1):
        series = 1.0 - u * (1.0 / n) * series
    return jnp.where(u < 0.125, u * series, 1.0 - jnp.exp(-u))


def packed(parts):
    value = jnp.concatenate(parts, axis=0)
    width = value.shape[1] // 2
    return jnp.concatenate([value[:, :width], value[:, width:]], axis=0).astype(BF16)


def unpacked(block):
    value = block.astype(F32)
    return jnp.concatenate([value[0:8], value[8:16]], axis=1)


def kernel(
    q_hbm, k_hbm, v_hbm, taps_hbm, rate_hbm, resid_hbm, w_hbm, o_ref,
    q_in, k_in, v_in, taps, rate_in, resid_in, w_own, w_par,
    q_ext, k_ext, v_ext, p_ext, p_group, halo_out, halo_in,
    rate, decay, coeff, heads, prefix, span, response, decay_b, gain_b, starts, local, q_feat,
    z_out, z_in, y_out, y_in, g_own, g_par, x_out, x_in, x_keep, h_out, h_in, unperm,
    in_sem, w_sem, wp_send, wp_recv, halo_sem, z_send, z_recv, y_send, y_recv, g_send, g_recv,
    x_send, x_recv, h_send, h_recv, ring_sem,
):
    rows, channels = q_in.shape
    rows_y, xs = y_in.shape[0], x_in.shape[2] + 1
    chunks, chunk = h_out.shape[0], h_out.shape[1]
    cols = h_out.shape[2]
    per = rows // BLOCK
    ctx, tp = lax.axis_index("ctx"), lax.axis_index("tp")
    y, z = ctx // RUN, ctx % RUN
    x, half, core = tp // 4, (tp // 2) % 2, tp % 2
    n_ctx = rows_y * RUN
    groups = [slice(g * LANES, (g + 1) * LANES) for g in range(channels // LANES)]

    def put(src, dst, send, recv, device):
        return pltpu.make_async_remote_copy(
            src_ref=src, dst_ref=dst, send_sem=send, recv_sem=recv, device_id=device, device_id_type=MESH
        )

    along_z = [(y * RUN + (z + d) % RUN, tp) for d in range(1, RUN)]
    along_y = [(((y + d) % rows_y) * RUN + z, tp) for d in range(1, rows_y)]
    along_x = [(ctx, ((x + d) % xs) * 4 + half * 2 + core) for d in range(1, xs)]
    other_core = (ctx, x * 4 + half * 2 + (1 - core))
    other_half = (ctx, x * 4 + (1 - half) * 2 + core)
    after, before = ((ctx + 1) % n_ctx, tp), ((ctx + n_ctx - 1) % n_ctx, tp)

    far_mate = (y * RUN + (z + RUN // 2) % RUN, other_half[1])
    near_y = [d for d in range(1, rows_y) if min(d, rows_y - d) <= 2]
    hop_y = [d for d in range(1, rows_y) if min(d, rows_y - d) == 2]
    told = along_z + along_x + [other_core, before, far_mate] + [along_y[d - 1] for d in near_y]

    loads = [
        pltpu.make_async_copy(src, dst, in_sem.at[i])
        for i, (src, dst) in enumerate(
            [(k_hbm, k_in), (v_hbm, v_in), (taps_hbm, taps), (rate_hbm, rate_in), (q_hbm, q_in), (resid_hbm, resid_in)]
        )
    ]
    for load in loads:
        load.start()

    barrier = pltpu.get_barrier_semaphore()
    for peer in told:
        pl.semaphore_signal(barrier, inc=1, device_id=peer, device_id_type=MESH)

    blocks = 2 * xs
    w_loads = [
        pltpu.make_async_copy(
            w_hbm.at[:, pl.ds(pl.multiple_of(b * 2 * cols + core * cols, cols), cols)], w_own.at[b], w_sem.at[b]
        )
        for b in range(blocks)
    ]
    w_shares = [
        put(
            w_hbm.at[:, pl.ds(pl.multiple_of(b * 2 * cols + (1 - core) * cols, cols), cols)],
            w_par.at[b], wp_send.at[b], wp_recv.at[b], other_core,
        )
        for b in range(blocks)
    ]

    for load in loads:
        load.wait()
    for w_load in w_loads:
        w_load.start()
    for ext in (k_ext, v_ext):
        ext[0:8, :] = jnp.zeros((8, channels), F32)

    for stream, ext in [(k_in, k_ext), (v_in, v_ext)]:
        for a in range(0, rows, 16):
            ext[8 + a : 24 + a, :] = stream[a : a + 16, :].astype(F32)

    def feature(ext, n, first, count):
        total = taps[n, 0:1, :] * ext[8 + first : 8 + first + count, :]
        total = total + taps[n, 1:2, :] * ext[7 + first : 7 + first + count, :]
        return total + taps[n, 2:3, :] * ext[6 + first : 6 + first + count, :]

    def product(first, count):
        value = feature(k_ext, 1, first, count) * feature(v_ext, 2, first, count)
        return value.astype(BF16).astype(F32)

    row_index = lax.broadcasted_iota(jnp.int32, (8, channels), 0)
    p_ext[0:8, :] = jnp.where(row_index < 2, 0.0, product(0, 8))
    for a in range(8, rows, 8):
        p_ext[a : a + 8, :] = product(a, 8)

    rate[...] = rate_in[...]
    decay[...] = jnp.exp(-rate[...])
    coeff[...] = resid_in[...] * jnp.sqrt(one_minus_exp(2.0 * rate[...]))

    step = decay[...]
    low, high = jnp.zeros_like(step), jnp.zeros_like(step)
    for t in range(rows // 2):
        if t % BLOCK == 0:
            prefix[t // BLOCK] = low
            prefix[(t + rows // 2) // BLOCK] = high
        low = step * low + p_ext[t : t + 1, :]
        high = step * high + p_ext[t + rows // 2 : t + rows // 2 + 1, :]
    middle, modes = low, step.shape[0]
    own = high + jnp.exp(rate[...] * (-0.5 * rows)) * middle
    head_gain = jnp.exp(rate[...] * (2.0 - rows))
    whole = jnp.exp(rate[...] * (-1.0 * rows))

    k_first, v_first = k_in[0:16, :].astype(F32), v_in[0:16, :].astype(F32)
    q_last, k_last, v_last = (stream[rows - 16 :, :].astype(F32)[14:16] for stream in (q_in, k_in, v_in))
    z_out[:, :channels] = own.astype(BF16)
    z_out[:, channels:] = packed([k_first[0:2], v_first[0:2], k_last, v_last])
    z_in[z] = z_out[...]
    halo_out[...] = packed([q_last, k_last, v_last, jnp.zeros_like(v_last)])
    pl.semaphore_wait(barrier, len(told))
    z_copies = [put(z_out, z_in.at[z], z_send.at[d - 1], z_recv.at[z], along_z[d - 1]) for d in range(1, RUN)]
    for copy in z_copies:
        copy.start()
    for d in hop_y:
        pl.semaphore_signal(ring_sem, inc=1, device_id=along_y[d - 1], device_id_type=MESH)
    halo = put(halo_out, halo_in, halo_sem.at[0], halo_sem.at[1], after)
    halo.start()
    for w_share in w_shares:
        w_share.start()

    def boundary(last, first):
        value = [1.0, 1.0]
        for n, old, new in ((1, 4, 0), (2, 6, 2)):
            tap = [taps[n, j : j + 1, :] for j in range(3)]
            line = [last[old : old + 1], last[old + 1 : old + 2], first[new : new + 1], first[new + 1 : new + 2]]
            for i in range(2):
                value[i] = value[i] * (tap[0] * line[i + 2] + tap[1] * line[i + 1] + tap[2] * line[i])
        value = [one.astype(BF16).astype(F32) for one in value]
        return step * value[0] + value[1]

    for b in range(1, per):
        span[b] = jnp.exp(rate[...] * (2.0 - BLOCK * b))
        if b > per // 2:
            prefix[b] = prefix[b] + jnp.exp(rate[...] * (1.0 * (per // 2 - b) * BLOCK)) * middle
    prefix[per // 2] = middle
    term = coeff[...]
    for k in range(BLOCK):
        response[k : k + 1, :] = jnp.sum(term, axis=0, keepdims=True)
        term = term * step
    first_gain = coeff[...] * step
    for g, lanes in enumerate(groups):
        for b in range(per):
            decay_b[g, pl.ds(b, modes, stride=per), :] = step[:, lanes]
            gain_b[g, pl.ds(b, modes, stride=per), :] = first_gain[:, lanes]

    before_me, total = jnp.zeros_like(step), jnp.zeros_like(step)
    edges = []
    for i in range(RUN):
        pl.when(z != i)(put(z_out, z_in.at[i], z_send.at[0], z_recv.at[i], along_z[0]).wait_recv)
        edges.append(unpacked(z_in[i, :, channels:]))
        value = z_in[i, :, :channels].astype(F32)
        if i > 0:
            value = value + head_gain * boundary(edges[i - 1], edges[i])
        before_me = jnp.where(i < z, whole * before_me + value, before_me)
        total = whole * total + value

    y_out[:, :channels] = total.astype(BF16)
    row_edges = [edges[0][0:2], edges[0][2:4], edges[RUN - 1][4:6], edges[RUN - 1][6:8]]
    y_out[:, channels:] = packed(row_edges)
    y_in[y] = y_out[...]
    pl.semaphore_wait(ring_sem, len(hop_y))
    y_copies = [put(y_out, y_in.at[y], y_send.at[d - 1], y_recv.at[y], along_y[d - 1]) for d in range(1, rows_y)]
    for d in sorted(range(1, rows_y), key=lambda d: (d != 1, -min(d, rows_y - d))):
        pl.when(y + d < rows_y)(y_copies[d - 1].start)
    halo.wait_recv()
    inside = jnp.where(ctx > 0, unpacked(halo_in[...]), 0.0)
    k_ext[6:8, :] = inside[2:4, :]
    v_ext[6:8, :] = inside[4:6, :]
    p_ext[0:8, :] = product(0, 8)
    heads[...] = step * p_ext[0:1, :] + p_ext[1:2, :]
    for g, lanes in enumerate(groups):
        q_ext[g, 6:8, :] = inside[0:2, lanes]
        for a in range(0, rows, 16):
            q_ext[g, 8 + a : 24 + a, :] = q_in[a : a + 16, lanes].astype(F32)
            p_group[g, a : a + 16, :] = p_ext[a : a + 16, lanes]
        for r in range(BLOCK):
            total = taps[0, 0:1, lanes] * q_ext[g, pl.ds(8 + r, per, stride=BLOCK), :]
            total = total + taps[0, 1:2, lanes] * q_ext[g, pl.ds(7 + r, per, stride=BLOCK), :]
            total = total + taps[0, 2:3, lanes] * q_ext[g, pl.ds(6 + r, per, stride=BLOCK), :]
            q_feat[r * per : (r + 1) * per, lanes] = total

    def convolve(group, carry):
        lanes = pl.ds(pl.multiple_of(group * LANES, LANES), LANES)
        inputs = [p_group[group, pl.ds(r, per, stride=BLOCK), :] for r in range(BLOCK)]
        for r in range(BLOCK):
            total = response[0:1, lanes] * inputs[r]
            for k in range(1, r + 1):
                total = total + response[k : k + 1, lanes] * inputs[r - k]
            local[r * per : (r + 1) * per, lanes] = total
        return carry

    lax.fori_loop(0, channels // LANES, convolve, 0)

    row_decay = jnp.exp(rate[...] * (-1.0 * rows * RUN))
    row_gain = jnp.exp(rate[...] * (2.0 - rows * RUN))
    my_gain = jnp.exp(rate[...] * (2.0 - rows * z.astype(F32)))
    state = jnp.zeros_like(step)
    last = jnp.zeros((8, channels), F32)
    row_heads = jnp.zeros_like(step)
    for i in range(rows_y):
        pl.when(i < y)(put(y_out, y_in.at[i], y_send.at[0], y_recv.at[i], along_y[0]).wait_recv)
        edge = unpacked(y_in[i, :, channels:])
        head = boundary(last, edge)
        row_heads = jnp.where(i == y, head, row_heads)
        value = row_decay * state + row_gain * head + y_in[i, :, :channels].astype(F32)
        state = jnp.where(i < y, value, state)
        last = edge
    state = jnp.where(z > 0, before_me + my_gain * (step * step * state + row_heads), state)
    second = step * step * state + heads[...]
    for b in range(per):
        if b > 0:
            state = prefix[b] + span[b] * second
        for g, lanes in enumerate(groups):
            starts[g, pl.ds(b, modes, stride=per), :] = state[:, lanes]

    steps = BLOCK // chunks
    g_copies, x_copies, h_copies = [], [], []
    for c in range(chunks):

        def gate(group, carry):
            lanes = pl.ds(pl.multiple_of(group * LANES, LANES), LANES)
            shape = (modes, per, LANES)
            ratio = decay_b[group].reshape(shape)
            term = starts[group].reshape(shape)
            if c == 0:
                term = term * gain_b[group].reshape(shape)
            for r in range(c * steps, (c + 1) * steps, 2):
                pair = []
                for one in (r, r + 1):
                    here = slice(one * per, (one + 1) * per)
                    value = local[here, lanes] + jnp.sum(term, axis=0)
                    term = term * ratio
                    pair.append(q_feat[here, lanes] * value.astype(BF16).astype(F32))
                g_own[r * per : (r + 2) * per, lanes] = jnp.concatenate(pair, axis=0).astype(BF16)
            if c + 1 < chunks:
                starts[group] = term.reshape(modes * per, LANES)
            return carry

        lax.fori_loop(0, channels // LANES, gate, 0)
        piece = pl.ds(c * chunk, chunk)
        copy = put(g_own.at[piece], g_par.at[piece], g_send.at[c], g_recv.at[c], other_core)
        copy.start()
        g_copies.append(copy)

    def share(b):
        value = jnp.dot(g_own[...], w_own[b], preferred_element_type=F32)
        return value + jnp.dot(g_par[...], w_par[b], preferred_element_type=F32)

    for w_load in w_loads:
        w_load.wait()
    for w_share in w_shares:
        w_share.wait()
    for c in range(chunks):
        g_copies[c].wait_recv()
    waiting = []
    for part, h in enumerate((1 - half, half)):
        copies = []
        for d in (2, 1, 3):
            to = (x + d) % xs
            value = share(to * 2 + h).astype(BF16)
            for c in range(chunks):
                x_out[part, c, d - 1] = value[c * chunk : (c + 1) * chunk]
                copy = put(
                    x_out.at[part, c, d - 1], x_in.at[part, c, d - 1],
                    x_send.at[part, c, d - 1], x_recv.at[part, c, d - 1], along_x[d - 1],
                )
                copies.append((c, copy))
            if part == 0:
                copies[-chunks][1].start()
        copies.sort(key=lambda item: item[0])
        for c, copy in copies:
            if part == 0 and c > 0:
                copy.start()
            if part == 1:
                waiting.append(copy)
            x_copies.append(copy)
        if part == 0:
            x_keep[0] = share(x * 2 + h)
    x_keep[1] = share(x * 2 + half)

    for part in range(2):
        for c in range(chunks):
            at = (part * chunks + c) * (xs - 1)
            for copy in x_copies[at : at + xs - 1]:
                copy.wait_recv()
            for a in range(0, chunk, 16):
                here = slice(c * chunk + a, c * chunk + a + 16)
                value = x_keep[part, here, :]
                for d in range(1, xs):
                    value = value + x_in[part, c, d - 1, a : a + 16, :].astype(F32)
                if part == 0:
                    h_out[c, a : a + 16, :] = value.astype(BF16)
                else:
                    x_keep[part, here, :] = value
            if part == 0:
                copy = put(h_out.at[c], h_in.at[c], h_send.at[c], h_recv.at[c], other_half)
                copy.start()
                h_copies.append(copy)
                if c == chunks - 1:
                    for copy in waiting:
                        copy.start()

    for c in range(chunks):
        h_copies[c].wait_recv()
        for a in range(0, chunk, 16):
            value = x_keep[1, c * chunk + a : c * chunk + a + 16, :] + h_in[c, a : a + 16, :].astype(F32)
            r = (c * chunk + a) // per
            for i in range(16 // per):
                for g in range(cols // LANES):
                    part = value[i * per : (i + 1) * per, g * LANES : (g + 1) * LANES]
                    unperm[g, pl.ds(r + i, per, stride=BLOCK), :] = part
    for copy in [halo] + z_copies + g_copies + x_copies + h_copies:
        copy.wait_send()
    for d in range(1, rows_y):
        pl.when(y + d < rows_y)(y_copies[d - 1].wait_send)
    for g in range(cols // LANES):
        o_ref[:, g * LANES : (g + 1) * LANES] = unperm[g].astype(BF16)


def solution(mesh):
    n_ctx, n_tp = mesh.shape["ctx"], mesh.shape["tp"]
    rows_y, xs = n_ctx // RUN, n_tp // 4
    chunks = 2

    def shards(queries, keys, values, short_taps, long_rates, long_resid, out_weight):
        rows, channels = queries.shape
        modes = long_rates.shape[1]
        out = out_weight.shape[1]
        cols = out // n_tp
        chunk = rows // chunks
        state = (modes, channels)
        message = (modes, channels + channels // 2)
        stream = pltpu.VMEM((rows, channels), BF16)
        sem = pltpu.SemaphoreType.DMA
        return pl.pallas_call(
            kernel,
            name="hyena",
            out_shape=pltpu.VMEM((rows, cols), BF16),
            in_specs=[pl.BlockSpec(memory_space=pltpu.HBM)] * 7,
            out_specs=pl.BlockSpec(memory_space=pltpu.VMEM),
            scratch_shapes=[
                stream, stream, stream,
                pltpu.VMEM(short_taps.shape, F32),
                pltpu.VMEM(state, F32),
                pltpu.VMEM(state, F32),
                pltpu.VMEM((2 * xs, channels, cols), BF16),
                pltpu.VMEM((2 * xs, channels, cols), BF16),
                pltpu.VMEM((channels // LANES, rows + 8, LANES), F32),
                pltpu.VMEM((rows + 8, channels), F32),
                pltpu.VMEM((rows + 8, channels), F32),
                pltpu.VMEM((rows, channels), F32),
                pltpu.VMEM((channels // LANES, rows, LANES), F32),
                pltpu.VMEM((16, channels // 2), BF16),
                pltpu.VMEM((16, channels // 2), BF16),
                pltpu.VMEM(state, F32),
                pltpu.VMEM(state, F32),
                pltpu.VMEM(state, F32),
                pltpu.VMEM(state, F32),
                pltpu.VMEM((rows // BLOCK,) + state, F32),
                pltpu.VMEM((rows // BLOCK,) + state, F32),
                pltpu.VMEM((BLOCK, channels), F32),
                pltpu.VMEM((channels // LANES, modes * (rows // BLOCK), LANES), F32),
                pltpu.VMEM((channels // LANES, modes * (rows // BLOCK), LANES), F32),
                pltpu.VMEM((channels // LANES, modes * (rows // BLOCK), LANES), F32),
                pltpu.VMEM((rows, channels), F32),
                pltpu.VMEM((rows, channels), F32),
                pltpu.VMEM(message, BF16),
                pltpu.VMEM((RUN,) + message, BF16),
                pltpu.VMEM(message, BF16),
                pltpu.VMEM((rows_y,) + message, BF16),
                stream, stream,
                pltpu.VMEM((2, chunks, xs - 1, chunk, cols), BF16),
                pltpu.VMEM((2, chunks, xs - 1, chunk, cols), BF16),
                pltpu.VMEM((2, rows, cols), F32),
                pltpu.VMEM((chunks, chunk, cols), BF16),
                pltpu.VMEM((chunks, chunk, cols), BF16),
                pltpu.VMEM((cols // LANES, rows, LANES), F32),
                sem((6,)),
                sem((2 * xs,)), sem((2 * xs,)), sem((2 * xs,)),
                sem((2,)),
                sem((RUN - 1,)), sem((RUN,)),
                sem((rows_y - 1,)), sem((rows_y,)),
                sem((chunks,)), sem((chunks,)),
                sem((2, chunks, xs - 1)), sem((2, chunks, xs - 1)),
                sem((chunks,)), sem((chunks,)),
                pltpu.SemaphoreType.REGULAR,
            ],
            compiler_params=pltpu.CompilerParams(
                collective_id=0, has_side_effects=True, vmem_limit_bytes=62 * 1024 * 1024
            ),
        )(queries, keys, values, short_taps, long_rates.T, long_resid.T, out_weight)

    return jax.shard_map(
        shards,
        mesh=mesh,
        in_specs=(
            P("ctx", "tp"),
            P("ctx", "tp"),
            P("ctx", "tp"),
            P(None, None, "tp"),
            P("tp", None),
            P("tp", None),
            P("tp", None),
        ),
        out_specs=P("ctx", "tp"),
        check_vma=False,
    )
```

```python
import jax
import jax.numpy as jnp
from jax import lax
from jax.experimental import pallas as pl
from jax.experimental.pallas import tpu as pltpu
from jax.sharding import PartitionSpec as P

MESH = pl.DeviceIdType.MESH
F32 = jnp.float32
BF16 = jnp.bfloat16
RUN = 8
BLOCK = 16
LANES = 128


def one_minus_exp(u):
    series = jnp.ones_like(u)
    for n in range(8, 1, -1):
        series = 1.0 - u * (1.0 / n) * series
    return jnp.where(u < 0.125, u * series, 1.0 - jnp.exp(-u))


def packed(parts):
    value = jnp.concatenate(parts, axis=0)
    width = value.shape[1] // 2
    return jnp.concatenate([value[:, :width], value[:, width:]], axis=0).astype(BF16)


def unpacked(block):
    value = block.astype(F32)
    return jnp.concatenate([value[0:8], value[8:16]], axis=1)


def kernel(
    q_hbm, k_hbm, v_hbm, taps_hbm, rate_hbm, resid_hbm, w_hbm, o_ref,
    q_in, k_in, v_in, taps, rate_in, resid_in, w_own, w_par,
    q_ext, k_ext, v_ext, p_ext, p_group, halo_out, halo_in,
    rate, decay, coeff, heads, prefix, span, response, decay_b, gain_b, starts, local, q_feat,
    z_out, z_in, y_out, y_in, g_own, g_par, x_out, x_in, x_keep, h_out, h_in, unperm,
    in_sem, w_sem, wp_send, wp_recv, halo_sem, z_send, z_recv, y_send, y_recv, g_send, g_recv,
    x_send, x_recv, h_send, h_recv, ring_sem,
):
    rows, channels = q_in.shape
    rows_y, xs = y_in.shape[0], x_in.shape[2] + 1
    chunks, chunk = h_out.shape[0], h_out.shape[1]
    cols = h_out.shape[2]
    per = rows // BLOCK
    ctx, tp = lax.axis_index("ctx"), lax.axis_index("tp")
    y, z = ctx // RUN, ctx % RUN
    x, half, core = tp // 4, (tp // 2) % 2, tp % 2
    n_ctx = rows_y * RUN
    groups = [slice(g * LANES, (g + 1) * LANES) for g in range(channels // LANES)]

    def put(src, dst, send, recv, device):
        return pltpu.make_async_remote_copy(
            src_ref=src, dst_ref=dst, send_sem=send, recv_sem=recv, device_id=device, device_id_type=MESH
        )

    along_z = [(y * RUN + (z + d) % RUN, tp) for d in range(1, RUN)]
    along_y = [(((y + d) % rows_y) * RUN + z, tp) for d in range(1, rows_y)]
    along_x = [(ctx, ((x + d) % xs) * 4 + half * 2 + core) for d in range(1, xs)]
    other_core = (ctx, x * 4 + half * 2 + (1 - core))
    other_half = (ctx, x * 4 + (1 - half) * 2 + core)
    after, before = ((ctx + 1) % n_ctx, tp), ((ctx + n_ctx - 1) % n_ctx, tp)

    far_mate = (y * RUN + (z + RUN // 2) % RUN, other_half[1])
    near_y = [d for d in range(1, rows_y) if min(d, rows_y - d) <= 2]
    far_y = [d for d in range(1, rows_y) if d not in near_y]
    hop_y = [d for d in range(1, rows_y) if min(d, rows_y - d) == 2]
    told = along_z + along_x + [other_core, before, far_mate] + [along_y[d - 1] for d in near_y]

    loads = [
        pltpu.make_async_copy(src, dst, in_sem.at[i])
        for i, (src, dst) in enumerate(
            [(k_hbm, k_in), (v_hbm, v_in), (taps_hbm, taps), (rate_hbm, rate_in), (q_hbm, q_in), (resid_hbm, resid_in)]
        )
    ]
    for load in loads:
        load.start()

    barrier = pltpu.get_barrier_semaphore()
    for peer in told:
        pl.semaphore_signal(barrier, inc=1, device_id=peer, device_id_type=MESH)

    @pl.when(z < RUN // 2)
    def _():
        for d in far_y:
            pl.semaphore_signal(barrier, inc=1, device_id=along_y[d - 1], device_id_type=MESH)


    blocks = 2 * xs
    w_loads = [
        pltpu.make_async_copy(
            w_hbm.at[:, pl.ds(pl.multiple_of(b * 2 * cols + core * cols, cols), cols)], w_own.at[b], w_sem.at[b]
        )
        for b in range(blocks)
    ]
    w_shares = [
        put(
            w_hbm.at[:, pl.ds(pl.multiple_of(b * 2 * cols + (1 - core) * cols, cols), cols)],
            w_par.at[b], wp_send.at[b], wp_recv.at[b], other_core,
        )
        for b in range(blocks)
    ]

    for load in loads:
        load.wait()
    for w_load in w_loads:
        w_load.start()
    for ext in (k_ext, v_ext):
        ext[0:8, :] = jnp.zeros((8, channels), F32)

    for stream, ext in [(k_in, k_ext), (v_in, v_ext)]:
        for a in range(0, rows, 16):
            ext[8 + a : 24 + a, :] = stream[a : a + 16, :].astype(F32)

    def feature(ext, n, first, count):
        total = taps[n, 0:1, :] * ext[8 + first : 8 + first + count, :]
        total = total + taps[n, 1:2, :] * ext[7 + first : 7 + first + count, :]
        return total + taps[n, 2:3, :] * ext[6 + first : 6 + first + count, :]

    def product(first, count):
        value = feature(k_ext, 1, first, count) * feature(v_ext, 2, first, count)
        return value.astype(BF16).astype(F32)

    row_index = lax.broadcasted_iota(jnp.int32, (8, channels), 0)
    p_ext[0:8, :] = jnp.where(row_index < 2, 0.0, product(0, 8))
    for a in range(8, rows, 8):
        p_ext[a : a + 8, :] = product(a, 8)

    rate[...] = rate_in[...]
    decay[...] = jnp.exp(-rate[...])
    coeff[...] = resid_in[...] * jnp.sqrt(one_minus_exp(2.0 * rate[...]))

    step = decay[...]
    low, high = jnp.zeros_like(step), jnp.zeros_like(step)
    for t in range(rows // 2):
        if t % BLOCK == 0:
            prefix[t // BLOCK] = low
            prefix[(t + rows // 2) // BLOCK] = high
        low = step * low + p_ext[t : t + 1, :]
        high = step * high + p_ext[t + rows // 2 : t + rows // 2 + 1, :]
    middle, modes = low, step.shape[0]
    own = high + jnp.exp(rate[...] * (-0.5 * rows)) * middle
    head_gain = jnp.exp(rate[...] * (2.0 - rows))
    whole = jnp.exp(rate[...] * (-1.0 * rows))

    k_first, v_first = k_in[0:16, :].astype(F32), v_in[0:16, :].astype(F32)
    q_last, k_last, v_last = (stream[rows - 16 :, :].astype(F32)[14:16] for stream in (q_in, k_in, v_in))
    z_out[:, :channels] = own.astype(BF16)
    z_out[:, channels:] = packed([k_first[0:2], v_first[0:2], k_last, v_last])
    z_in[z] = z_out[...]
    halo_out[...] = packed([q_last, k_last, v_last, jnp.zeros_like(v_last)])
    pl.semaphore_wait(barrier, len(told) + jnp.where(z < RUN // 2, len(far_y), 0))
    z_copies = [put(z_out, z_in.at[z], z_send.at[d - 1], z_recv.at[z], along_z[d - 1]) for d in range(1, RUN)]
    for copy in z_copies:
        copy.start()

    @pl.when(z >= RUN // 2)
    def _():
        for d in hop_y:
            pl.semaphore_signal(ring_sem, inc=1, device_id=along_y[d - 1], device_id_type=MESH)

    halo = put(halo_out, halo_in, halo_sem.at[0], halo_sem.at[1], after)
    halo.start()
    for w_share in w_shares:
        w_share.start()

    def boundary(last, first):
        value = [1.0, 1.0]
        for n, old, new in ((1, 4, 0), (2, 6, 2)):
            tap = [taps[n, j : j + 1, :] for j in range(3)]
            line = [last[old : old + 1], last[old + 1 : old + 2], first[new : new + 1], first[new + 1 : new + 2]]
            for i in range(2):
                value[i] = value[i] * (tap[0] * line[i + 2] + tap[1] * line[i + 1] + tap[2] * line[i])
        value = [one.astype(BF16).astype(F32) for one in value]
        return step * value[0] + value[1]

    for b in range(1, per):
        span[b] = jnp.exp(rate[...] * (2.0 - BLOCK * b))
        if b > per // 2:
            prefix[b] = prefix[b] + jnp.exp(rate[...] * (1.0 * (per // 2 - b) * BLOCK)) * middle
    prefix[per // 2] = middle
    term = coeff[...]
    for k in range(BLOCK):
        response[k : k + 1, :] = jnp.sum(term, axis=0, keepdims=True)
        term = term * step
    first_gain = coeff[...] * step
    for g, lanes in enumerate(groups):
        for b in range(per):
            decay_b[g, pl.ds(b, modes, stride=per), :] = step[:, lanes]
            gain_b[g, pl.ds(b, modes, stride=per), :] = first_gain[:, lanes]

    before_me, total = jnp.zeros_like(step), jnp.zeros_like(step)
    edges = []
    for i in range(RUN):
        pl.when(z != i)(put(z_out, z_in.at[i], z_send.at[0], z_recv.at[i], along_z[0]).wait_recv)
        edges.append(unpacked(z_in[i, :, channels:]))
        value = z_in[i, :, :channels].astype(F32)
        if i > 0:
            value = value + head_gain * boundary(edges[i - 1], edges[i])
        before_me = jnp.where(i < z, whole * before_me + value, before_me)
        total = whole * total + value

    y_out[:, :channels] = total.astype(BF16)
    row_edges = [edges[0][0:2], edges[0][2:4], edges[RUN - 1][4:6], edges[RUN - 1][6:8]]
    y_out[:, channels:] = packed(row_edges)
    y_in[y] = y_out[...]
    @pl.when(z >= RUN // 2)
    def _():
        pl.semaphore_wait(ring_sem, len(hop_y))

    y_copies = [put(y_out, y_in.at[y], y_send.at[d - 1], y_recv.at[y], along_y[d - 1]) for d in range(1, rows_y)]
    for d in sorted(range(1, rows_y), key=lambda d: (d != 1, -min(d, rows_y - d))):
        pl.when(y + d < rows_y)(y_copies[d - 1].start)
    halo.wait_recv()
    inside = jnp.where(ctx > 0, unpacked(halo_in[...]), 0.0)
    k_ext[6:8, :] = inside[2:4, :]
    v_ext[6:8, :] = inside[4:6, :]
    p_ext[0:8, :] = product(0, 8)
    heads[...] = step * p_ext[0:1, :] + p_ext[1:2, :]
    for g, lanes in enumerate(groups):
        q_ext[g, 6:8, :] = inside[0:2, lanes]
        for a in range(0, rows, 16):
            q_ext[g, 8 + a : 24 + a, :] = q_in[a : a + 16, lanes].astype(F32)
            p_group[g, a : a + 16, :] = p_ext[a : a + 16, lanes]
        for r in range(BLOCK):
            total = taps[0, 0:1, lanes] * q_ext[g, pl.ds(8 + r, per, stride=BLOCK), :]
            total = total + taps[0, 1:2, lanes] * q_ext[g, pl.ds(7 + r, per, stride=BLOCK), :]
            total = total + taps[0, 2:3, lanes] * q_ext[g, pl.ds(6 + r, per, stride=BLOCK), :]
            q_feat[r * per : (r + 1) * per, lanes] = total

    def convolve(group, carry):
        lanes = pl.ds(pl.multiple_of(group * LANES, LANES), LANES)
        inputs = [p_group[group, pl.ds(r, per, stride=BLOCK), :] for r in range(BLOCK)]
        for r in range(BLOCK):
            total = response[0:1, lanes] * inputs[r]
            for k in range(1, r + 1):
                total = total + response[k : k + 1, lanes] * inputs[r - k]
            local[r * per : (r + 1) * per, lanes] = total
        return carry

    lax.fori_loop(0, channels // LANES, convolve, 0)

    row_decay = jnp.exp(rate[...] * (-1.0 * rows * RUN))
    row_gain = jnp.exp(rate[...] * (2.0 - rows * RUN))
    my_gain = jnp.exp(rate[...] * (2.0 - rows * z.astype(F32)))
    state = jnp.zeros_like(step)
    last = jnp.zeros((8, channels), F32)
    row_heads = jnp.zeros_like(step)
    for i in range(rows_y):
        pl.when(i < y)(put(y_out, y_in.at[i], y_send.at[0], y_recv.at[i], along_y[0]).wait_recv)
        edge = unpacked(y_in[i, :, channels:])
        head = boundary(last, edge)
        row_heads = jnp.where(i == y, head, row_heads)
        value = row_decay * state + row_gain * head + y_in[i, :, :channels].astype(F32)
        state = jnp.where(i < y, value, state)
        last = edge
    state = jnp.where(z > 0, before_me + my_gain * (step * step * state + row_heads), state)
    second = step * step * state + heads[...]
    for b in range(per):
        if b > 0:
            state = prefix[b] + span[b] * second
        for g, lanes in enumerate(groups):
            starts[g, pl.ds(b, modes, stride=per), :] = state[:, lanes]

    steps = BLOCK // chunks
    g_copies, x_copies, h_copies = [], [], []
    for c in range(chunks):

        def gate(group, carry):
            lanes = pl.ds(pl.multiple_of(group * LANES, LANES), LANES)
            shape = (modes, per, LANES)
            ratio = decay_b[group].reshape(shape)
            term = starts[group].reshape(shape)
            if c == 0:
                term = term * gain_b[group].reshape(shape)
            for r in range(c * steps, (c + 1) * steps, 2):
                pair = []
                for one in (r, r + 1):
                    here = slice(one * per, (one + 1) * per)
                    value = local[here, lanes] + jnp.sum(term, axis=0)
                    term = term * ratio
                    pair.append(q_feat[here, lanes] * value.astype(BF16).astype(F32))
                g_own[r * per : (r + 2) * per, lanes] = jnp.concatenate(pair, axis=0).astype(BF16)
            if c + 1 < chunks:
                starts[group] = term.reshape(modes * per, LANES)
            return carry

        lax.fori_loop(0, channels // LANES, gate, 0)
        piece = pl.ds(c * chunk, chunk)
        copy = put(g_own.at[piece], g_par.at[piece], g_send.at[c], g_recv.at[c], other_core)
        copy.start()
        g_copies.append(copy)

    def share(b):
        value = jnp.dot(g_own[...], w_own[b], preferred_element_type=F32)
        return value + jnp.dot(g_par[...], w_par[b], preferred_element_type=F32)

    for w_load in w_loads:
        w_load.wait()
    for w_share in w_shares:
        w_share.wait()
    for c in range(chunks):
        g_copies[c].wait_recv()
    waiting = []
    for part, h in enumerate((1 - half, half)):
        copies = []
        for d in (2, 1, 3):
            to = (x + d) % xs
            value = share(to * 2 + h).astype(BF16)
            for c in range(chunks):
                x_out[part, c, d - 1] = value[c * chunk : (c + 1) * chunk]
                copy = put(
                    x_out.at[part, c, d - 1], x_in.at[part, c, d - 1],
                    x_send.at[part, c, d - 1], x_recv.at[part, c, d - 1], along_x[d - 1],
                )
                copies.append((c, copy))
            if part == 0:
                copies[-chunks][1].start()
        copies.sort(key=lambda item: item[0])
        for c, copy in copies:
            if part == 0 and c > 0:
                copy.start()
            if part == 1:
                waiting.append(copy)
            x_copies.append(copy)
        if part == 0:
            x_keep[0] = share(x * 2 + h)
    x_keep[1] = share(x * 2 + half)

    for part in range(2):
        for c in range(chunks):
            at = (part * chunks + c) * (xs - 1)
            for copy in x_copies[at : at + xs - 1]:
                copy.wait_recv()
            for a in range(0, chunk, 16):
                here = slice(c * chunk + a, c * chunk + a + 16)
                value = x_keep[part, here, :]
                for d in range(1, xs):
                    value = value + x_in[part, c, d - 1, a : a + 16, :].astype(F32)
                if part == 0:
                    h_out[c, a : a + 16, :] = value.astype(BF16)
                else:
                    x_keep[part, here, :] = value
            if part == 0:
                copy = put(h_out.at[c], h_in.at[c], h_send.at[c], h_recv.at[c], other_half)
                copy.start()
                h_copies.append(copy)
                if c == chunks - 1:
                    for copy in waiting:
                        copy.start()

    for c in range(chunks):
        h_copies[c].wait_recv()
        for a in range(0, chunk, 16):
            value = x_keep[1, c * chunk + a : c * chunk + a + 16, :] + h_in[c, a : a + 16, :].astype(F32)
            r = (c * chunk + a) // per
            for i in range(16 // per):
                for g in range(cols // LANES):
                    part = value[i * per : (i + 1) * per, g * LANES : (g + 1) * LANES]
                    unperm[g, pl.ds(r + i, per, stride=BLOCK), :] = part
    for copy in [halo] + z_copies + g_copies + x_copies + h_copies:
        copy.wait_send()
    for d in range(1, rows_y):
        pl.when(y + d < rows_y)(y_copies[d - 1].wait_send)
    for g in range(cols // LANES):
        o_ref[:, g * LANES : (g + 1) * LANES] = unperm[g].astype(BF16)


def solution(mesh):
    n_ctx, n_tp = mesh.shape["ctx"], mesh.shape["tp"]
    rows_y, xs = n_ctx // RUN, n_tp // 4
    chunks = 2

    def shards(queries, keys, values, short_taps, long_rates, long_resid, out_weight):
        rows, channels = queries.shape
        modes = long_rates.shape[1]
        out = out_weight.shape[1]
        cols = out // n_tp
        chunk = rows // chunks
        state = (modes, channels)
        message = (modes, channels + channels // 2)
        stream = pltpu.VMEM((rows, channels), BF16)
        sem = pltpu.SemaphoreType.DMA
        return pl.pallas_call(
            kernel,
            name="hyena",
            out_shape=pltpu.VMEM((rows, cols), BF16),
            in_specs=[pl.BlockSpec(memory_space=pltpu.HBM)] * 7,
            out_specs=pl.BlockSpec(memory_space=pltpu.VMEM),
            scratch_shapes=[
                stream, stream, stream,
                pltpu.VMEM(short_taps.shape, F32),
                pltpu.VMEM(state, F32),
                pltpu.VMEM(state, F32),
                pltpu.VMEM((2 * xs, channels, cols), BF16),
                pltpu.VMEM((2 * xs, channels, cols), BF16),
                pltpu.VMEM((channels // LANES, rows + 8, LANES), F32),
                pltpu.VMEM((rows + 8, channels), F32),
                pltpu.VMEM((rows + 8, channels), F32),
                pltpu.VMEM((rows, channels), F32),
                pltpu.VMEM((channels // LANES, rows, LANES), F32),
                pltpu.VMEM((16, channels // 2), BF16),
                pltpu.VMEM((16, channels // 2), BF16),
                pltpu.VMEM(state, F32),
                pltpu.VMEM(state, F32),
                pltpu.VMEM(state, F32),
                pltpu.VMEM(state, F32),
                pltpu.VMEM((rows // BLOCK,) + state, F32),
                pltpu.VMEM((rows // BLOCK,) + state, F32),
                pltpu.VMEM((BLOCK, channels), F32),
                pltpu.VMEM((channels // LANES, modes * (rows // BLOCK), LANES), F32),
                pltpu.VMEM((channels // LANES, modes * (rows // BLOCK), LANES), F32),
                pltpu.VMEM((channels // LANES, modes * (rows // BLOCK), LANES), F32),
                pltpu.VMEM((rows, channels), F32),
                pltpu.VMEM((rows, channels), F32),
                pltpu.VMEM(message, BF16),
                pltpu.VMEM((RUN,) + message, BF16),
                pltpu.VMEM(message, BF16),
                pltpu.VMEM((rows_y,) + message, BF16),
                stream, stream,
                pltpu.VMEM((2, chunks, xs - 1, chunk, cols), BF16),
                pltpu.VMEM((2, chunks, xs - 1, chunk, cols), BF16),
                pltpu.VMEM((2, rows, cols), F32),
                pltpu.VMEM((chunks, chunk, cols), BF16),
                pltpu.VMEM((chunks, chunk, cols), BF16),
                pltpu.VMEM((cols // LANES, rows, LANES), F32),
                sem((6,)),
                sem((2 * xs,)), sem((2 * xs,)), sem((2 * xs,)),
                sem((2,)),
                sem((RUN - 1,)), sem((RUN,)),
                sem((rows_y - 1,)), sem((rows_y,)),
                sem((chunks,)), sem((chunks,)),
                sem((2, chunks, xs - 1)), sem((2, chunks, xs - 1)),
                sem((chunks,)), sem((chunks,)),
                pltpu.SemaphoreType.REGULAR,
            ],
            compiler_params=pltpu.CompilerParams(
                collective_id=0, has_side_effects=True, vmem_limit_bytes=62 * 1024 * 1024
            ),
        )(queries, keys, values, short_taps, long_rates.T, long_resid.T, out_weight)

    return jax.shard_map(
        shards,
        mesh=mesh,
        in_specs=(
            P("ctx", "tp"),
            P("ctx", "tp"),
            P("ctx", "tp"),
            P(None, None, "tp"),
            P("tp", None),
            P("tp", None),
            P("tp", None),
        ),
        out_specs=P("ctx", "tp"),
        check_vma=False,
    )
```
